256 devices in a mesh: leaf: 32 (over z, x), grp: 8 (over y, core).
Axes of the slice: x: 4, y: 4, z: 8, core: 2. Of those that a mesh axis runs over, the one named last changes fastest.
Arguments:
- hidden_states: bfloat16 [8, 4096, 2560], P('grp', 'leaf'), may hold values from -6 to 6
- query_rows: bfloat16 [8, 4096, 5120], P('grp', 'leaf'), may hold values from -170 to 170
- key_rows: bfloat16 [8, 4096, 512], P('grp', 'leaf'), may hold values from -7 to 7
- value_weight: bfloat16 [2560, 512], P(('leaf', 'grp')), may hold values from -0.125 to 0.125
- parent_links: int32 [8, 32], P('grp', 'leaf'), may hold values from -1 to 30, as said below
- out_grad: bfloat16 [8, 4096, 5120], P('grp', 'leaf'), may hold values from -6 to 6
Outputs:
- attended: bfloat16 [8, 4096, 5120], P('grp', 'leaf')
- query_grad: bfloat16 [8, 4096, 5120], P('grp', 'leaf')
- key_grad: bfloat16 [8, 4096, 512], P('grp', 'leaf')
- hidden_grad: bfloat16 [8, 4096, 2560], P('grp', 'leaf')
- weight_grad: float32 [2560, 512], P(('leaf', 'grp'))
The draws below stay inside these ranges and needn't reach their ends.
Inputs may be any that keep to these rules, and one draw needn't show every extreme that they name: `parent_links`: entry 0 of each tree is -1 and every other entry names a lower index; no segment has more than 4 children, every segment is at most 3 steps from segment 0, and in every tree some segment is exactly 3 steps from it and segment 0 has exactly 4 children.
All inputs are finite; a program needn't handle non-finite values.
Results may differ from the reference program's by a relative error of at most 0.028.
Values may be sent and summed in bfloat16 or wider, within the bound.
No kernel may reach another device: no remote copies, remote signals or barrier semaphores. Data moves between devices by JAX's collectives and lax.ppermute only.
A program may use at most 128 MiB of HBM per device.

```python
import jax
import jax.numpy as jnp
from jax import lax

D = 2560
HQ = 40
HK = 4
DH = 128
SEG = 128
TOKENS = 4096
N_LEAF = 32
N_GRP = 8


def shared_keys(key):
    return jnp.clip(jax.random.normal(key, (N_GRP, N_LEAF * SEG, HK * DH), jnp.float32), -6.0, 6.0)


def draw_key_rows(key, part):
    base_rows = shared_keys(key)
    return base_rows.astype(jnp.bfloat16)


def draw_query_rows(key, part):
    key = jax.random.fold_in(key, 5)
    fresh_rows = jnp.clip(jax.random.normal(key, (N_GRP, N_LEAF * SEG, HQ * DH), jnp.float32), -6.0, 6.0)
    return fresh_rows.astype(jnp.bfloat16)


def build_tree(key):
    node_ids = jnp.arange(N_LEAF, dtype=jnp.int32)
    ranking = jax.random.randint(key, (N_LEAF, N_LEAF), 0, 65536, dtype=jnp.int32) * 128 + node_ids[None, :]
    first_pick = jax.random.randint(jax.random.fold_in(key, 2), (), 1, 5, dtype=jnp.int32)
    parent_of = jnp.where((node_ids >= 1) & (node_ids <= 4), 0, -1).astype(jnp.int32)
    parent_of = parent_of.at[5].set(first_pick).at[6].set(5)
    depth_of = jnp.where(node_ids == 0, 0, jnp.where(node_ids <= 4, 1, jnp.where(node_ids == 5, 2, jnp.where(node_ids == 6, 3, 9)))).astype(jnp.int32)
    child_count = jnp.zeros((N_LEAF,), jnp.int32).at[0].set(4).at[first_pick].add(1).at[5].add(1)

    def step(node_index, carry):
        parent_now, depth_now, count_now = carry
        eligible = (node_ids < node_index) & (depth_now >= 1) & (depth_now <= 2) & (count_now < 4)
        ranked = jnp.where(eligible, ranking[node_index], -1)
        chosen = jnp.argmax(ranked).astype(jnp.int32)
        return (parent_now.at[node_index].set(chosen), depth_now.at[node_index].set(depth_now[chosen] + 1), count_now.at[chosen].add(1))
    parent_of, depth_of, child_count = lax.fori_loop(7, N_LEAF, step, (parent_of, depth_of, child_count))
    return parent_of.astype(jnp.int32)


def draw_parent_links(key, part):
    key = jax.random.fold_in(key, 11)
    return jax.vmap(build_tree)(jax.random.split(key, N_GRP))


def spiked(array, key, source, target, parts, factor):
    owner, partner = [(jnp.arange(array.shape[dim]) // (array.shape[dim] // parts)).reshape([-1 if axis == dim else 1 for axis in range(array.ndim)]) for dim in (source, target)]
    chosen = jax.random.permutation(key, parts)[partner]
    strong = (owner == chosen) | (owner == (partner + parts // 2) % parts)
    return jnp.where(strong, factor * array, array)


def block_scale(own_key, shape, shards, smallest, largest):
    factor_of, own = 1.0, jax.random.fold_in(own_key, 6)
    for position, shards_of in shards:
        steps = jnp.exp(jax.random.uniform(jax.random.fold_in(own, position), (shards_of,), jnp.float32, smallest / len(shards), largest / len(shards)))
        factor_of = factor_of * jnp.repeat(steps, shape[position] // shards_of).reshape([-1 if axis == position else 1 for axis in range(len(shape))])
    return factor_of


def normal_values(key, dims, spread, reach, cuts=(), kind=jnp.bfloat16):
    gain = block_scale(key, dims, cuts, -0.22, 0.18) if cuts else 1.0
    drawn = jax.random.normal(key, dims, jnp.float32) * spread * gain
    return jnp.minimum(jnp.maximum(drawn, -reach), reach).astype(kind)


def heavy_noise(own_key, dims, spread, bound, pieces, heavy, held_as=jnp.bfloat16):
    drawn = spread * jax.random.normal(own_key, dims, jnp.float32)
    if pieces:
        drawn = drawn * block_scale(own_key, dims, pieces, -0.22, 0.18)
    return jnp.clip(spiked(drawn, jax.random.fold_in(own_key, 3), *heavy), -bound, bound).astype(held_as)


def setup_inputs(seed: int = 0) -> dict:
    streams_of = jax.random.split(jax.random.key(seed), 7)
    return {
        "hidden_states": heavy_noise(streams_of[0], (N_GRP, TOKENS, D), 1.0, 6.0, ((0, 8), (1, 32)), (1, 2, 32, 2.75)),
        "query_rows": draw_query_rows(jax.random.fold_in(streams_of[6], 71), 0),
        "key_rows": draw_key_rows(jax.random.fold_in(streams_of[6], 71), 0),
        "value_weight": normal_values(streams_of[3], (D, HK * DH), D ** -0.5, 0.125, ((0, 256),)),
        "parent_links": draw_parent_links(jax.random.fold_in(streams_of[6], 71), 0),
        "out_grad": normal_values(streams_of[5], (N_GRP, TOKENS, HQ * DH), 1.0, 6.0, ((0, 8), (1, 32))),
    }


def chain_slots(parent_list, own_index):
    total = parent_list.shape[0]

    def parent_of(node_index):
        hit = jnp.arange(total, dtype=jnp.int32) == node_index
        found = jnp.sum(jnp.where(hit, parent_list, 0)).astype(jnp.int32)
        return jnp.where(node_index >= 0, found, -1).astype(jnp.int32)

    first = parent_of(own_index)
    second = parent_of(first)
    third = parent_of(second)
    return jnp.stack([first, second, third]).astype(jnp.int32)


def key_mask(ancestors, segment_len):
    valid = jnp.concatenate([ancestors >= 0, jnp.ones((1,), bool)])
    block_ok = jnp.repeat(valid, segment_len)[None, :]
    row_ids = jnp.arange(segment_len, dtype=jnp.int32)[:, None]
    col_ids = jnp.arange(4 * segment_len, dtype=jnp.int32)[None, :]
    causal = (col_ids < 3 * segment_len) | (col_ids - 3 * segment_len <= row_ids)
    return block_ok & causal


def segment_pass(query_seg, key_all, value_all, grad_seg, visible):
    segment_len = query_seg.shape[0]
    groups = HQ // HK
    scale_factor = 1.0 / (DH ** 0.5)
    query_heads = query_seg.astype(jnp.float32).reshape(segment_len, HK, groups, DH)
    key_heads = key_all.astype(jnp.float32).reshape(-1, HK, DH)
    value_heads = value_all.astype(jnp.float32).reshape(-1, HK, DH)
    grad_heads = grad_seg.astype(jnp.float32).reshape(segment_len, HK, groups, DH)
    scores = jnp.einsum('rhgd,khd->hgrk', query_heads, key_heads) * scale_factor
    scores = jnp.where(visible, scores, -1e30)
    row_max = jnp.max(scores, axis=-1, keepdims=True)
    weights_exp = jnp.where(visible, jnp.exp(scores - row_max), 0.0)
    probs = weights_exp / jnp.sum(weights_exp, axis=-1, keepdims=True)
    probs_low = probs.astype(jnp.bfloat16).astype(jnp.float32)
    output = jnp.einsum('hgrk,khd->rhgd', probs_low, value_heads).reshape(segment_len, HQ * DH).astype(jnp.bfloat16)
    dprobs = jnp.einsum('rhgd,khd->hgrk', grad_heads, value_heads)
    delta = jnp.sum(probs * dprobs, axis=-1, keepdims=True)
    dscores = (probs * (dprobs - delta)).astype(jnp.bfloat16).astype(jnp.float32)
    query_grad = (jnp.einsum('hgrk,khd->rhgd', dscores, key_heads) * scale_factor).reshape(segment_len, HQ * DH).astype(jnp.bfloat16)
    key_part = jnp.einsum('hgrk,rhgd->khd', dscores, query_heads) * scale_factor
    value_part = jnp.einsum('hgrk,rhgd->khd', probs_low, grad_heads)
    grad_term = jnp.concatenate([key_part.reshape(-1, HK * DH), value_part.reshape(-1, HK * DH)], axis=1)
    return output, query_grad, grad_term


def reference(hidden_states, query_rows, key_rows, value_weight, parent_links, out_grad):
    key_width = HK * DH

    def one_group(inputs):
        hidden_g, query_g, key_g, parent_g, grad_g = inputs
        values = jnp.dot(hidden_g, value_weight, preferred_element_type=jnp.float32).astype(jnp.bfloat16)
        key_value = jnp.concatenate([key_g, values], axis=1)

        def step(carry, seg_index):
            ancestors = chain_slots(parent_g, seg_index)
            blocks = [lax.dynamic_slice_in_dim(key_value, (jnp.maximum(ancestors[i], 0) * SEG).astype(jnp.int32), SEG, 0) for i in range(3)]
            own_start = (seg_index * SEG).astype(jnp.int32)
            blocks.append(lax.dynamic_slice_in_dim(key_value, own_start, SEG, 0))
            gathered = jnp.concatenate(blocks, axis=0)
            query_seg = lax.dynamic_slice_in_dim(query_g, own_start, SEG, 0)
            grad_seg = lax.dynamic_slice_in_dim(grad_g, own_start, SEG, 0)
            output, query_grad, grad_term = segment_pass(query_seg, gathered[:, :key_width], gathered[:, key_width:], grad_seg, key_mask(ancestors, SEG))
            term_low = lax.optimization_barrier(grad_term.astype(jnp.bfloat16)).astype(jnp.float32)
            owners = jnp.concatenate([ancestors, seg_index[None]]).astype(jnp.int32)
            for slot_index in range(4):
                start = (jnp.maximum(owners[slot_index], 0) * SEG).astype(jnp.int32)
                current = lax.dynamic_slice_in_dim(carry, start, SEG, 0)
                carry = lax.dynamic_update_slice_in_dim(carry, current + term_low[slot_index * SEG:(slot_index + 1) * SEG], start, 0)
            return carry, (output, query_grad)

        sums, (outputs, query_grads) = lax.scan(step, jnp.zeros((N_LEAF * SEG, 2 * key_width), jnp.float32), jnp.arange(N_LEAF, dtype=jnp.int32))
        key_grad = sums[:, :key_width].astype(jnp.bfloat16)
        value_grad = sums[:, key_width:].astype(jnp.bfloat16)
        hidden_grad = jnp.dot(value_grad, value_weight.T, preferred_element_type=jnp.float32).astype(jnp.bfloat16)
        weight_part = jnp.dot(hidden_g.T, value_grad, preferred_element_type=jnp.float32)
        return outputs.reshape(N_LEAF * SEG, HQ * DH), query_grads.reshape(N_LEAF * SEG, HQ * DH), key_grad, hidden_grad, weight_part

    results = lax.map(one_group, (hidden_states, query_rows, key_rows, parent_links, out_grad))
    weight_grad = jnp.sum(results[4], axis=0)
    return results[0], results[1], results[2], results[3], weight_grad
```

```python
import functools

import jax
import jax.numpy as jnp
from jax import lax
from jax.experimental import pallas as pl
from jax.experimental.pallas import tpu as pltpu
from jax.sharding import PartitionSpec as P

HQ = 40
HK = 4
DH = 128
GROUPS = HQ // HK
SLOTS = 3
TILE = 16
LOG2E = 1.4426950408889634
BF = jnp.bfloat16
F32 = jnp.float32
VMEM_LIMIT = 56 * 1024 * 1024


def ancestors_of(parents, node):
    first = parents[node]
    second = jnp.where(first >= 0, parents[jnp.maximum(first, 0)], -1)
    third = jnp.where(second >= 0, parents[jnp.maximum(second, 0)], -1)
    return (first, second, third)


def fetch_kernel(parents, held, sent):
    for node in range(sent.shape[0]):
        for slot, owner in enumerate(ancestors_of(parents, node)):
            sent[node, slot * TILE : (slot + 1) * TILE, :] = held[jnp.maximum(owner, 0), 0:TILE, :]


def add_up(parents, held, total):
    nodes = held.shape[0]
    total[...] = jnp.zeros_like(total)
    for node in range(nodes):
        for slot, owner in enumerate(ancestors_of(parents, node)):
            target = jnp.where(owner >= 0, owner, nodes)
            total[target] += held[node, slot * TILE : (slot + 1) * TILE, :].astype(F32)


def value_kernel(parents, held, sent, total):
    add_up(parents, held, total)
    for node in range(held.shape[0]):
        for slot, owner in enumerate(ancestors_of(parents, node)):
            sent[node, slot * TILE : (slot + 1) * TILE, :] = held[
                jnp.maximum(owner, 0), SLOTS * TILE : (SLOTS + 1) * TILE, :
            ]
        sent[node, SLOTS * TILE : (SLOTS + 1) * TILE, :] = total[node].astype(BF)


def key_kernel(parents, held, sent, total):
    add_up(parents, held, total)
    for node in range(held.shape[0]):
        sent[node] = total[node].astype(BF)


def whole(shape):
    return pl.BlockSpec(shape, lambda *_: (0,) * len(shape))


def route(kernel, parents, held, rows, with_total):
    nodes = held.shape[0]
    return pl.pallas_call(
        kernel,
        out_shape=jax.ShapeDtypeStruct((nodes, rows, DH), BF),
        in_specs=[
            pl.BlockSpec(memory_space=pltpu.SMEM),
            pl.BlockSpec(memory_space=pltpu.VMEM),
        ],
        out_specs=pl.BlockSpec(memory_space=pltpu.VMEM),
        scratch_shapes=[pltpu.VMEM((nodes + 1, TILE, DH), F32)] if with_total else [],
        compiler_params=pltpu.CompilerParams(vmem_limit_bytes=VMEM_LIMIT),
        cost_estimate=pl.CostEstimate(flops=0, bytes_accessed=2 * held.size * 2, transcendentals=0),
    )(parents, held)


def rows_of(pieces, own):
    parts = [
        pieces[:, 0, slot * TILE : (slot + 1) * TILE, :].reshape(-1, DH) for slot in range(SLOTS)
    ]
    return jnp.concatenate(parts + [own[...]], axis=0)


def put_rows(pieces, own, rows):
    seg = own.shape[0]
    for slot in range(SLOTS):
        block = rows[slot * seg : (slot + 1) * seg, :]
        pieces[:, 0, slot * TILE : (slot + 1) * TILE, :] = block.reshape(-1, TILE, DH).astype(BF)
    own[...] = rows[SLOTS * seg :, :].astype(BF)


def pair(block, index):
    return jnp.concatenate(
        [block[:, (2 * index + i) * DH : (2 * index + i + 1) * DH] for i in range(2)], axis=0
    )


def put_pair(block, index, rows):
    seg = block.shape[0]
    for i in range(2):
        block[:, (2 * index + i) * DH : (2 * index + i + 1) * DH] = rows[
            i * seg : (i + 1) * seg, :
        ].astype(BF)


def dot(lhs, rhs, left, right):
    return lax.dot_general(lhs, rhs, (((left,), (right,)), ((), ())), preferred_element_type=F32)


def probs_kernel(valid, query, grad, key_pieces, key_own, probs, value_pieces, value_own, bias):
    seg = query.shape[0]

    @pl.when(pl.program_id(0) == 0)
    def _():
        key_ids = lax.broadcasted_iota(jnp.int32, (seg, 2 * seg), 0)
        query_ids = lax.broadcasted_iota(jnp.int32, (seg, 2 * seg), 1) % seg
        for slot in range(SLOTS):
            level = jnp.where(valid[slot] >= 0, 0.0, -1e30).astype(F32)
            bias[slot * seg : (slot + 1) * seg, :] = jnp.full((seg, 2 * seg), level, F32)
        bias[SLOTS * seg :, :] = jnp.where(key_ids <= query_ids, 0.0, -1e30)

    keys = rows_of(key_pieces, key_own)
    total = jnp.zeros((keys.shape[0], DH), F32)
    for index in range(GROUPS // 2):
        scores = dot(keys, pair(query, index), 1, 1) * (LOG2E / DH**0.5) + bias[...]
        weight = jnp.exp2(scores - jnp.max(scores, axis=0, keepdims=True))
        prob = weight * (1.0 / jnp.sum(weight, axis=0, keepdims=True))
        probs[0, :, index * 2 * seg : (index + 1) * 2 * seg] = prob
        total += dot(prob.astype(BF), pair(grad, index), 1, 0)
    put_rows(value_pieces, value_own, total)


def grads_kernel(
    query, grad, probs, key_pieces, key_own, value_pieces, value_own,
    output, query_grad, grad_pieces, grad_own,
):
    seg = query.shape[0]
    keys = rows_of(key_pieces, key_own)
    values = rows_of(value_pieces, value_own)
    total = jnp.zeros((keys.shape[0], DH), F32)
    for index in range(GROUPS // 2):
        prob = probs[0, :, index * 2 * seg : (index + 1) * 2 * seg]
        dprob = dot(values, pair(grad, index), 1, 1)
        delta = jnp.sum(prob * dprob, axis=0, keepdims=True)
        dscore = (prob * (dprob - delta)).astype(BF)
        total += dot(dscore, pair(query, index), 1, 0)
        put_pair(output, index, dot(prob.astype(BF), values, 0, 0))
        put_pair(query_grad, index, dot(dscore, keys, 0, 0) * (1.0 / DH**0.5))
    put_rows(grad_pieces, grad_own, total * (1.0 / DH**0.5))


def attention(kernel, valid, arrays, outs, scratch, flops, transcendentals):
    def spec(shape):
        if len(shape) == 4:
            return pl.BlockSpec((shape[0], 1) + shape[2:], lambda h: (0, h, 0, 0))
        if len(shape) == 3:
            return pl.BlockSpec((1,) + shape[1:], lambda h: (h, 0, 0))
        return pl.BlockSpec((shape[0], shape[1] // HK), lambda h: (0, h))

    lead = [] if valid is None else [valid]
    moved = sum(a.size * a.dtype.itemsize for a in arrays) + sum(
        o.size * o.dtype.itemsize for o in outs
    )
    return pl.pallas_call(
        kernel,
        grid=(HK,),
        out_shape=outs,
        in_specs=[pl.BlockSpec(memory_space=pltpu.SMEM)] * len(lead)
        + [spec(a.shape) for a in arrays],
        out_specs=[spec(o.shape) for o in outs],
        scratch_shapes=scratch,
        compiler_params=pltpu.CompilerParams(vmem_limit_bytes=VMEM_LIMIT),
        cost_estimate=pl.CostEstimate(
            flops=flops, bytes_accessed=moved, transcendentals=transcendentals
        ),
    )(*lead, *arrays)


def to_pieces(rows):
    seg, width = rows.shape
    split = rows.reshape(seg // TILE, TILE, width // DH, DH).transpose(0, 2, 1, 3)
    return split.reshape(-1, TILE, DH)


def from_pieces(pieces):
    split = pieces.reshape(-1, HK, TILE, DH).transpose(0, 2, 1, 3)
    return split.reshape(-1, HK * DH)


def swap(array):
    return lax.all_to_all(array, "leaf", 0, 0, tiled=True)


def shards(n_leaf, n_grp, hidden_states, query_rows, key_rows, value_weight, parent_links, out_grad):
    hidden, query, keys, grad = hidden_states[0], query_rows[0], key_rows[0], out_grad[0]
    seg, width = keys.shape
    depth = hidden.shape[1]
    own_rows = value_weight.shape[0]
    blocks = seg // TILE
    shape = jax.ShapeDtypeStruct
    flops = 2 * seg * 4 * seg * DH * HQ

    columns = hidden.reshape(seg, n_leaf, n_grp, own_rows).transpose(0, 2, 1, 3).reshape(seg, depth)

    weight_rows = own_rows * width // DH
    pad = (-weight_rows) % TILE or TILE
    first = jnp.concatenate(
        [
            to_pieces(keys),
            jnp.broadcast_to(value_weight.reshape(1, weight_rows, DH), (n_leaf, weight_rows, DH)),
            jnp.broadcast_to(parent_links.astype(BF)[:, :, None], (n_leaf, pad, DH)),
        ],
        axis=1,
    )
    first = swap(first)
    parents = first[:, TILE + weight_rows, 0].astype(jnp.int32)
    weight = first[:, TILE : TILE + weight_rows, :].reshape(n_leaf * own_rows, width)
    weight = lax.all_gather(weight, "grp", axis=0, tiled=True)

    key_pieces = swap(route(fetch_kernel, parents, first[:, :TILE, :], SLOTS * TILE, False))
    key_pieces = key_pieces.reshape(blocks, HK, SLOTS * TILE, DH)
    valid = jnp.stack(ancestors_of(parents, lax.axis_index("leaf")))
    probs, value_terms, value_term_own = attention(
        probs_kernel,
        valid,
        [query, grad, key_pieces, keys],
        [
            shape((HK, 4 * seg, GROUPS * seg), F32),
            shape((blocks, HK, SLOTS * TILE, DH), BF),
            shape((seg, width), BF),
        ],
        [pltpu.VMEM((4 * seg, 2 * seg), F32)],
        2 * flops,
        HQ * seg * 4 * seg,
    )

    values = jnp.dot(columns, weight, preferred_element_type=F32).astype(BF)
    third = jnp.concatenate(
        [value_terms.reshape(-1, SLOTS * TILE, DH), to_pieces(values)], axis=1
    )
    third = swap(third)

    fourth = swap(route(value_kernel, parents, third, (SLOTS + 1) * TILE, True))
    value_grad = (
        from_pieces(fourth[:, SLOTS * TILE :, :]).astype(F32) + value_term_own.astype(F32)
    ).astype(BF)
    weight_part = dot(columns, value_grad, 0, 0).astype(BF)
    weight_part = lax.psum_scatter(weight_part, "grp", scatter_dimension=0, tiled=True)
    output, query_grad, key_terms, key_term_own = attention(
        grads_kernel,
        None,
        [
            query, grad, probs, key_pieces, keys,
            fourth.reshape(blocks, HK, (SLOTS + 1) * TILE, DH), values,
        ],
        [
            shape((seg, HQ * DH), BF),
            shape((seg, HQ * DH), BF),
            shape((blocks, HK, SLOTS * TILE, DH), BF),
            shape((seg, width), BF),
        ],
        [],
        4 * flops,
        0,
    )
    hidden_grad = dot(value_grad, weight, 1, 1).astype(BF)
    hidden_grad = hidden_grad.reshape(seg, n_grp, n_leaf, own_rows).transpose(0, 2, 1, 3)
    hidden_grad = hidden_grad.reshape(seg, depth)

    fifth = swap(key_terms.reshape(-1, SLOTS * TILE, DH))

    sixth = jnp.concatenate(
        [
            route(key_kernel, parents, fifth, TILE, True),
            weight_part.reshape(n_leaf, weight_rows, DH).astype(BF),
        ],
        axis=1,
    )
    sixth = swap(sixth)
    key_grad = (
        from_pieces(sixth[:, :TILE, :]).astype(F32) + key_term_own.astype(F32)
    ).astype(BF)
    weight_grad = jnp.sum(sixth[:, TILE:, :].astype(F32), axis=0).reshape(own_rows, width)
    return (output[None], query_grad[None], key_grad[None], hidden_grad[None], weight_grad)


def solution(mesh):
    rows = P("grp", "leaf", None)
    spread = P(("leaf", "grp"), None)
    return jax.shard_map(
        functools.partial(shards, mesh.shape["leaf"], mesh.shape["grp"]),
        mesh=mesh,
        in_specs=(rows, rows, rows, spread, P("grp", "leaf"), rows),
        out_specs=(rows, rows, rows, rows, spread),
        check_vma=False,
    )
```

```python
import functools

import jax
import jax.numpy as jnp
import numpy as np
from jax import lax
from jax.experimental import pallas as pl
from jax.experimental.pallas import tpu as pltpu
from jax.sharding import PartitionSpec as P

HQ = 40
HK = 4
DH = 128
GROUPS = HQ // HK
SLOTS = 3
TILE = 16
LOG2E = 1.4426950408889634
BF = jnp.bfloat16
F32 = jnp.float32
VMEM_LIMIT = 56 * 1024 * 1024


def spread_rows(n_leaf, own_rows):
    leaf, head, row = (x.ravel() for x in np.indices((8, HK, own_rows)))
    source = (head * 8 + leaf) * own_rows + row
    return (source[:, None] == np.arange(source.size)[None, :]).astype(np.float32)


def pack_kernel(own_rows, parent, keys, weight, sent, rows):
    count = HK * own_rows
    rows[...] = jnp.full(rows.shape, parent[0, 0].astype(F32), F32)
    for head in range(HK):
        rows[head * own_rows : (head + 1) * own_rows, :] = weight[
            :, head * DH : (head + 1) * DH
        ].astype(F32)
    common = rows[...].astype(BF)
    for piece in range(sent.shape[0]):
        block, head = piece // HK, piece % HK
        sent[piece, 0:TILE, :] = keys[block * TILE : (block + 1) * TILE, head * DH : (head + 1) * DH]
        sent[piece, TILE:, :] = common


def fetch_kernel(own_rows, held, select, sent, weight, table, wide, parents, arrived):
    nodes = held.shape[0]
    count = HK * own_rows
    tail = held[:, held.shape[1] - TILE :, :].astype(F32)
    wide[...] = jnp.max(tail[:, TILE // 2 :, :], axis=1).astype(jnp.int32)
    copy = pltpu.make_async_copy(wide, parents, arrived)
    copy.start()
    for group in range(nodes // 8):
        part = held[group * 8 : (group + 1) * 8, TILE:, :].astype(F32)[:, :count, :]
        part = part.reshape(8 * count, DH).astype(BF)
        moved = dot(select[...], part, 0, 0).astype(BF)
        for head in range(HK):
            weight[
                group * 8 * own_rows : (group + 1) * 8 * own_rows, head * DH : (head + 1) * DH
            ] = moved[head * 8 * own_rows : (head + 1) * 8 * own_rows, :]
    copy.wait()
    for node in range(nodes):
        parent = parents[node, 0]
        above = table[jnp.maximum(parent, 0)] if node > 0 else -1
        deep = jnp.logical_and(parent > 0, above >= 0)
        table[node] = jnp.where(deep, above, jnp.where(parent > 0, parent, -1))
        table[nodes + node] = jnp.where(deep, parent, -1)
    for node in range(nodes):
        sent[node, 0:TILE, :] = held[0, 0:TILE, :]
        for slot in range(1, SLOTS):
            owner = jnp.maximum(table[(slot - 1) * nodes + node], 0)
            sent[node, slot * TILE : (slot + 1) * TILE, :] = held[owner, 0:TILE, :]


def add_up(table, held, totals):
    nodes = held.shape[0]
    for total in totals:
        total[...] = jnp.zeros_like(total)
    root = jnp.zeros((TILE, DH), F32)
    for node in range(nodes):
        root = root + held[node, 0:TILE, :].astype(F32)
        for slot in range(1, SLOTS):
            owner = jnp.maximum(table[(slot - 1) * nodes + node], 0)
            totals[slot - 1][owner] += held[node, slot * TILE : (slot + 1) * TILE, :].astype(F32)
    totals[0][0] += root


def value_kernel(table, held, sent, *totals):
    nodes = held.shape[0]
    values = slice(SLOTS * TILE, (SLOTS + 1) * TILE)
    add_up(table, held, totals)
    for node in range(nodes):
        sent[node, 0:TILE, :] = held[0, values, :]
        for slot in range(1, SLOTS):
            owner = jnp.maximum(table[(slot - 1) * nodes + node], 0)
            sent[node, slot * TILE : (slot + 1) * TILE, :] = held[owner, values, :]
        sent[node, values, :] = (totals[0][node] + totals[1][node]).astype(BF)


def key_kernel(own_rows, table, held, part, select, sent, *totals):
    nodes = held.shape[0]
    count = HK * own_rows
    add_up(table, held, totals)
    for node in range(nodes):
        sent[node, 0:TILE, :] = (totals[0][node] + totals[1][node]).astype(BF)
    for group in range(nodes // 8):
        rows = part[group * 8 * own_rows : (group + 1) * 8 * own_rows, :]
        rows = jnp.concatenate([rows[:, h * DH : (h + 1) * DH] for h in range(HK)], axis=0)
        moved = dot(select[...], rows, 1, 0).reshape(8, count, DH)
        fill = jnp.zeros((8, sent.shape[1] - TILE - count, DH), F32)
        sent[group * 8 : (group + 1) * 8, TILE:, :] = jnp.concatenate(
            [moved, fill], axis=1
        ).astype(BF)


def last_kernel(own_rows, held, key_own, key_grad, weight_grad, rows):
    for piece in range(held.shape[0]):
        block, head = piece // HK, piece % HK
        at = (slice(block * TILE, (block + 1) * TILE), slice(head * DH, (head + 1) * DH))
        key_grad[at] = (held[piece, 0:TILE, :].astype(F32) + key_own[at].astype(F32)).astype(BF)
    rows[...] = jnp.sum(held[:, TILE:, :].astype(F32), axis=0)
    for head in range(HK):
        weight_grad[:, head * DH : (head + 1) * DH] = rows[
            head * own_rows : (head + 1) * own_rows, :
        ]


def project_kernel(pieces, own, columns, value_grad, part):
    @pl.when(pl.program_id(0) == 0)
    def _():
        for block in range(pieces.shape[0]):
            for head in range(HK):
                at = (slice(block * TILE, (block + 1) * TILE), slice(head * DH, (head + 1) * DH))
                value_grad[at] = (
                    pieces[block, head].astype(F32) + own[at].astype(F32)
                ).astype(BF)

    part[...] = dot(columns[...], value_grad[...], 1, 0).astype(BF)


def plain(kernel, arrays, outs, scratch=(), scalars=0, scalar_outs=0, flops=0):
    smem, vmem = pl.BlockSpec(memory_space=pltpu.SMEM), pl.BlockSpec(memory_space=pltpu.VMEM)
    moved = sum(a.size * a.dtype.itemsize for a in list(arrays) + list(outs))
    return pl.pallas_call(
        kernel,
        out_shape=outs,
        in_specs=[smem] * scalars + [vmem] * (len(arrays) - scalars),
        out_specs=[vmem] * (len(outs) - scalar_outs) + [smem] * scalar_outs,
        scratch_shapes=list(scratch),
        compiler_params=pltpu.CompilerParams(vmem_limit_bytes=VMEM_LIMIT),
        cost_estimate=pl.CostEstimate(flops=flops, bytes_accessed=moved, transcendentals=0),
    )(*arrays)


def rows_of(pieces, own):
    parts = [
        pieces[:, 0, slot * TILE : (slot + 1) * TILE, :].reshape(-1, DH) for slot in range(SLOTS)
    ]
    return jnp.concatenate(parts + [own[...]], axis=0)


def put_rows(pieces, own, rows):
    seg = own.shape[0]
    for slot in range(SLOTS):
        block = rows[slot * seg : (slot + 1) * seg, :]
        pieces[:, 0, slot * TILE : (slot + 1) * TILE, :] = block.reshape(-1, TILE, DH).astype(BF)
    own[...] = rows[SLOTS * seg :, :].astype(BF)


def pair(block, index):
    return jnp.concatenate(
        [block[:, (2 * index + i) * DH : (2 * index + i + 1) * DH] for i in range(2)], axis=0
    )


def put_pair(block, index, rows):
    seg = block.shape[0]
    for i in range(2):
        block[:, (2 * index + i) * DH : (2 * index + i + 1) * DH] = rows[
            i * seg : (i + 1) * seg, :
        ].astype(BF)


def dot(lhs, rhs, left, right):
    return lax.dot_general(lhs, rhs, (((left,), (right,)), ((), ())), preferred_element_type=F32)


def probs_kernel(table, own, query, grad, key_pieces, key_own, probs, value_pieces, value_own, bias):
    seg = query.shape[0]

    @pl.when(pl.program_id(0) == 0)
    def _():
        key_ids = lax.broadcasted_iota(jnp.int32, (seg, 2 * seg), 0)
        query_ids = lax.broadcasted_iota(jnp.int32, (seg, 2 * seg), 1) % seg
        bias[...] = jnp.where(key_ids <= query_ids, 0.0, -1e30)

    nodes = table.shape[0] // (SLOTS - 1)
    present = [own[0] > 0] + [table[slot * nodes + own[0]] >= 0 for slot in range(SLOTS - 1)]
    levels = [jnp.where(here, 0.0, -1e30).astype(F32) for here in present]
    keys = rows_of(key_pieces, key_own)
    total = jnp.zeros((keys.shape[0], DH), F32)
    for index in range(GROUPS // 2):
        scores = dot(keys, pair(query, index), 1, 1) * (LOG2E / DH**0.5)
        scores = jnp.concatenate(
            [scores[slot * seg : (slot + 1) * seg, :] + levels[slot] for slot in range(SLOTS)]
            + [scores[SLOTS * seg :, :] + bias[...]],
            axis=0,
        )
        weight = jnp.exp2(scores - jnp.max(scores, axis=0, keepdims=True))
        prob = weight * (1.0 / jnp.sum(weight, axis=0, keepdims=True))
        probs[0, :, index * 2 * seg : (index + 1) * 2 * seg] = prob
        total += dot(prob.astype(BF), pair(grad, index), 1, 0)
    put_rows(value_pieces, value_own, total)


def grads_kernel(
    query, grad, probs, key_pieces, key_own, value_pieces, value_own,
    output, query_grad, grad_pieces, grad_own,
):
    seg = query.shape[0]
    keys = rows_of(key_pieces, key_own)
    values = rows_of(value_pieces, value_own)
    keys_t, values_t = keys.T, values.T
    total = jnp.zeros((keys.shape[0], DH), F32)
    for index in range(GROUPS // 2):
        prob = probs[0, :, index * 2 * seg : (index + 1) * 2 * seg]
        dprob = dot(values, pair(grad, index), 1, 1)
        delta = jnp.sum(prob * dprob, axis=0, keepdims=True)
        dscore = (prob * (dprob - delta)).astype(BF)
        total += dot(dscore, pair(query, index), 1, 0)
        put_pair(output, index, dot(values_t, prob.astype(BF), 1, 0).astype(BF).T)
        put_pair(query_grad, index, (dot(keys_t, dscore, 1, 0) * (1.0 / DH**0.5)).astype(BF).T)
    put_rows(grad_pieces, grad_own, total * (1.0 / DH**0.5))


def attention(kernel, lead, arrays, outs, scratch, flops, transcendentals):
    def spec(shape):
        if len(shape) == 4:
            return pl.BlockSpec((shape[0], 1) + shape[2:], lambda h: (0, h, 0, 0))
        if len(shape) == 3:
            return pl.BlockSpec((1,) + shape[1:], lambda h: (h, 0, 0))
        return pl.BlockSpec((shape[0], shape[1] // HK), lambda h: (0, h))

    moved = sum(a.size * a.dtype.itemsize for a in arrays) + sum(
        o.size * o.dtype.itemsize for o in outs
    )
    return pl.pallas_call(
        kernel,
        grid=(HK,),
        out_shape=outs,
        in_specs=[pl.BlockSpec(memory_space=pltpu.SMEM)] * len(lead)
        + [spec(a.shape) for a in arrays],
        out_specs=[spec(o.shape) for o in outs],
        scratch_shapes=scratch,
        compiler_params=pltpu.CompilerParams(vmem_limit_bytes=VMEM_LIMIT),
        cost_estimate=pl.CostEstimate(
            flops=flops, bytes_accessed=moved, transcendentals=transcendentals
        ),
    )(*lead, *arrays)


def project(pieces, own, columns, steps=2):
    blocks = pieces.shape[0]
    seg, width = own.shape
    depth = columns.shape[0]
    return pl.pallas_call(
        project_kernel,
        grid=(steps,),
        out_shape=[
            jax.ShapeDtypeStruct((seg, width), BF),
            jax.ShapeDtypeStruct((depth, width), BF),
        ],
        in_specs=[
            pl.BlockSpec((blocks, HK, TILE, DH), lambda i: (0, 0, SLOTS, 0)),
            pl.BlockSpec((seg, width), lambda i: (0, 0)),
            pl.BlockSpec((depth // steps, seg), lambda i: (i, 0)),
        ],
        out_specs=[
            pl.BlockSpec((seg, width), lambda i: (0, 0)),
            pl.BlockSpec((depth // steps, width), lambda i: (i, 0)),
        ],
        compiler_params=pltpu.CompilerParams(vmem_limit_bytes=VMEM_LIMIT),
        cost_estimate=pl.CostEstimate(
            flops=2 * seg * width * depth,
            bytes_accessed=2 * depth * (width + seg),
            transcendentals=0,
        ),
    )(pieces, own, columns)


def to_pieces(rows):
    seg, width = rows.shape
    split = rows.reshape(seg // TILE, TILE, width // DH, DH).transpose(0, 2, 1, 3)
    return split.reshape(-1, TILE, DH)


def swap(array):
    return lax.all_to_all(array, "leaf", 0, 0, tiled=True)


def shards(n_leaf, n_grp, hidden_states, query_rows, key_rows, value_weight, parent_links, out_grad):
    hidden, query, keys, grad = hidden_states[0], query_rows[0], key_rows[0], out_grad[0]
    seg, width = keys.shape
    depth = hidden.shape[1]
    own_rows = value_weight.shape[0]
    blocks = seg // TILE
    tail = -(-(HK * own_rows + TILE // 2) // TILE) * TILE
    shape = jax.ShapeDtypeStruct
    flops = 2 * seg * 4 * seg * DH * HQ
    select = jnp.asarray(spread_rows(n_leaf, own_rows), BF)
    totals = [pltpu.VMEM((n_leaf, TILE, DH), F32)] * (SLOTS - 1)
    slots = SLOTS * TILE

    columns = hidden.T.reshape(n_leaf, n_grp, own_rows, seg).transpose(1, 0, 2, 3)
    columns = columns.reshape(depth, seg)

    (first,) = plain(
        functools.partial(pack_kernel, own_rows),
        [parent_links, keys, value_weight],
        [shape((n_leaf, TILE + tail, DH), BF)],
        [pltpu.VMEM((tail, DH), F32)],
        scalars=1,
    )
    first = swap(first)

    second, weight, table = plain(
        functools.partial(fetch_kernel, own_rows),
        [first, select],
        [
            shape((n_leaf, slots, DH), BF),
            shape((n_leaf * own_rows, width), BF),
            shape(((SLOTS - 1) * n_leaf,), jnp.int32),
        ],
        [
            pltpu.VMEM((n_leaf, DH), jnp.int32),
            pltpu.SMEM((n_leaf, DH), jnp.int32),
            pltpu.SemaphoreType.DMA,
        ],
        scalar_outs=1,
    )
    weight = lax.all_gather(weight, "grp", axis=0, tiled=True)
    key_pieces = swap(second).reshape(blocks, HK, slots, DH)
    probs, value_terms, value_term_own = attention(
        probs_kernel,
        [table, lax.axis_index("leaf").astype(jnp.int32).reshape(1)],
        [query, grad, key_pieces, keys],
        [
            shape((HK, 4 * seg, GROUPS * seg), F32),
            shape((blocks, HK, slots, DH), BF),
            shape((seg, width), BF),
        ],
        [pltpu.VMEM((seg, 2 * seg), F32)],
        2 * flops,
        HQ * seg * 4 * seg,
    )

    values = dot(columns, weight, 0, 0).astype(BF)
    third = jnp.concatenate([value_terms.reshape(-1, slots, DH), to_pieces(values)], axis=1)
    third = swap(third)

    (fourth,) = plain(
        value_kernel, [table, third], [shape((n_leaf, slots + TILE, DH), BF)], totals, scalars=1
    )
    fourth = swap(fourth).reshape(blocks, HK, slots + TILE, DH)
    value_grad, weight_part = project(fourth, value_term_own, columns)
    weight_part = lax.psum_scatter(weight_part, "grp", scatter_dimension=0, tiled=True)
    output, query_grad, key_terms, key_term_own = attention(
        grads_kernel,
        [],
        [query, grad, probs, key_pieces, keys, fourth, values],
        [
            shape((seg, HQ * DH), BF),
            shape((seg, HQ * DH), BF),
            shape((blocks, HK, slots, DH), BF),
            shape((seg, width), BF),
        ],
        [],
        4 * flops,
        0,
    )
    hidden_grad = dot(value_grad, weight, 1, 1).astype(BF)
    hidden_grad = hidden_grad.reshape(seg, n_grp, n_leaf, own_rows).transpose(0, 2, 1, 3)
    hidden_grad = hidden_grad.reshape(seg, depth)

    fifth = swap(key_terms.reshape(-1, slots, DH))

    (sixth,) = plain(
        functools.partial(key_kernel, own_rows),
        [table, fifth, weight_part, select],
        [shape((n_leaf, TILE + tail, DH), BF)],
        totals,
        scalars=1,
    )
    sixth = swap(sixth)
    key_grad, weight_grad = plain(
        functools.partial(last_kernel, own_rows),
        [sixth, key_term_own],
        [shape((seg, width), BF), shape((own_rows, width), F32)],
        [pltpu.VMEM((tail, DH), F32)],
    )
    return (output[None], query_grad[None], key_grad[None], hidden_grad[None], weight_grad)


def solution(mesh):
    rows = P("grp", "leaf", None)
    spread = P(("leaf", "grp"), None)
    return jax.shard_map(
        functools.partial(shards, mesh.shape["leaf"], mesh.shape["grp"]),
        mesh=mesh,
        in_specs=(rows, rows, rows, spread, P("grp", "leaf"), rows),
        out_specs=(rows, rows, rows, rows, spread),
        check_vma=False,
    )
```

```python
import functools

import jax
import jax.numpy as jnp
import numpy as np
from jax import lax
from jax.experimental import pallas as pl
from jax.experimental.pallas import tpu as pltpu
from jax.sharding import PartitionSpec as P

HQ = 40
HK = 4
DH = 128
GROUPS = HQ // HK
SLOTS = 3
TILE = 16
LOG2E = 1.4426950408889634
BF = jnp.bfloat16
F32 = jnp.float32
VMEM_LIMIT = 28 * 1024 * 1024


def spread_rows(n_leaf, own_rows):
    leaf, head, row = (x.ravel() for x in np.indices((8, HK, own_rows)))
    source = (head * 8 + leaf) * own_rows + row
    return (source[:, None] == np.arange(source.size)[None, :]).astype(np.float32)


def pack_kernel(own_rows, parent, keys, weight, sent, rows):
    count = HK * own_rows
    rows[...] = jnp.full(rows.shape, parent[0, 0].astype(F32), F32)
    for head in range(HK):
        rows[head * own_rows : (head + 1) * own_rows, :] = weight[
            :, head * DH : (head + 1) * DH
        ].astype(F32)
    common = rows[...].astype(BF)
    for piece in range(sent.shape[0]):
        block, head = piece // HK, piece % HK
        sent[piece, 0:TILE, :] = keys[block * TILE : (block + 1) * TILE, head * DH : (head + 1) * DH]
        sent[piece, TILE:, :] = common


def weight_kernel(own_rows, held, select, weight):
    count = HK * own_rows
    for group in range(held.shape[0] // 8):
        part = held[group * 8 : (group + 1) * 8, TILE:, :].astype(F32)[:, :count, :]
        part = part.reshape(8 * count, DH).astype(BF)
        moved = dot(select[...], part, 0, 0).astype(BF)
        for head in range(HK):
            weight[
                group * 8 * own_rows : (group + 1) * 8 * own_rows, head * DH : (head + 1) * DH
            ] = moved[head * 8 * own_rows : (head + 1) * 8 * own_rows, :]


def fetch_kernel(held, sent, table, wide, parents, arrived):
    nodes = held.shape[0]
    tail = held[:, held.shape[1] - TILE :, :].astype(F32)
    wide[...] = jnp.max(tail[:, TILE // 2 :, :], axis=1).astype(jnp.int32)
    copy = pltpu.make_async_copy(wide, parents, arrived)
    copy.start()
    for node in range(nodes):
        sent[node, 0:TILE, :] = held[0, 0:TILE, :]
    copy.wait()
    for node in range(nodes):
        parent = parents[node, 0]
        above = table[jnp.maximum(parent, 0)] if node > 0 else -1
        deep = jnp.logical_and(parent > 0, above >= 0)
        table[node] = jnp.where(deep, above, jnp.where(parent > 0, parent, -1))
        table[nodes + node] = jnp.where(deep, parent, -1)
    for node in range(nodes):
        for slot in range(1, SLOTS):
            owner = jnp.maximum(table[(slot - 1) * nodes + node], 0)
            sent[node, slot * TILE : (slot + 1) * TILE, :] = held[owner, 0:TILE, :]


def add_up(table, held, totals):
    nodes = held.shape[0]
    for total in totals:
        total[...] = jnp.zeros_like(total)
    root = jnp.zeros((TILE, DH), F32)
    for node in range(nodes):
        root = root + held[node, 0:TILE, :].astype(F32)
        for slot in range(1, SLOTS):
            owner = jnp.maximum(table[(slot - 1) * nodes + node], 0)
            totals[slot - 1][owner] += held[node, slot * TILE : (slot + 1) * TILE, :].astype(F32)
    totals[0][0] += root


def value_kernel(table, held, sent, *totals):
    nodes = held.shape[0]
    values = slice(SLOTS * TILE, (SLOTS + 1) * TILE)
    add_up(table, held, totals)
    for node in range(nodes):
        sent[node, 0:TILE, :] = held[0, values, :]
        for slot in range(1, SLOTS):
            owner = jnp.maximum(table[(slot - 1) * nodes + node], 0)
            sent[node, slot * TILE : (slot + 1) * TILE, :] = held[owner, values, :]
        sent[node, values, :] = (totals[0][node] + totals[1][node]).astype(BF)


def key_kernel(table, held, sums, *totals):
    add_up(table, held, totals)
    for node in range(held.shape[0]):
        sums[node] = (totals[0][node] + totals[1][node]).astype(BF)


def join_kernel(own_rows, sums, part, select, sent):
    count = HK * own_rows
    sent[:, 0:TILE, :] = sums[...]
    for group in range(sent.shape[0] // 8):
        rows = part[group * 8 * own_rows : (group + 1) * 8 * own_rows, :]
        rows = jnp.concatenate([rows[:, h * DH : (h + 1) * DH] for h in range(HK)], axis=0)
        moved = dot(select[...], rows, 1, 0).reshape(8, count, DH)
        fill = jnp.zeros((8, sent.shape[1] - TILE - count, DH), F32)
        sent[group * 8 : (group + 1) * 8, TILE:, :] = jnp.concatenate(
            [moved, fill], axis=1
        ).astype(BF)


def last_kernel(own_rows, held, key_own, key_grad, weight_grad, rows):
    for piece in range(held.shape[0]):
        block, head = piece // HK, piece % HK
        at = (slice(block * TILE, (block + 1) * TILE), slice(head * DH, (head + 1) * DH))
        key_grad[at] = (held[piece, 0:TILE, :].astype(F32) + key_own[at].astype(F32)).astype(BF)
    rows[...] = jnp.sum(held[:, TILE:, :].astype(F32), axis=0)
    for head in range(HK):
        weight_grad[:, head * DH : (head + 1) * DH] = rows[
            head * own_rows : (head + 1) * own_rows, :
        ]


def project_kernel(pieces, own, columns, value_grad, part):
    @pl.when(pl.program_id(0) == 0)
    def _():
        for block in range(pieces.shape[0]):
            for head in range(HK):
                at = (slice(block * TILE, (block + 1) * TILE), slice(head * DH, (head + 1) * DH))
                value_grad[at] = (
                    pieces[block, head].astype(F32) + own[at].astype(F32)
                ).astype(BF)

    part[...] = dot(columns[...], value_grad[...], 1, 0).astype(BF)


def plain(kernel, arrays, outs, scratch=(), scalars=0, scalar_outs=0, flops=0):
    smem, vmem = pl.BlockSpec(memory_space=pltpu.SMEM), pl.BlockSpec(memory_space=pltpu.VMEM)
    moved = sum(a.size * a.dtype.itemsize for a in list(arrays) + list(outs))
    return pl.pallas_call(
        kernel,
        out_shape=outs,
        in_specs=[smem] * scalars + [vmem] * (len(arrays) - scalars),
        out_specs=[vmem] * (len(outs) - scalar_outs) + [smem] * scalar_outs,
        scratch_shapes=list(scratch),
        compiler_params=pltpu.CompilerParams(vmem_limit_bytes=VMEM_LIMIT),
        cost_estimate=pl.CostEstimate(flops=flops, bytes_accessed=moved, transcendentals=0),
    )(*arrays)


def rows_of(pieces, own):
    parts = [
        pieces[:, 0, slot * TILE : (slot + 1) * TILE, :].reshape(-1, DH) for slot in range(SLOTS)
    ]
    return jnp.concatenate(parts + [own[...]], axis=0)


def put_rows(pieces, own, rows):
    seg = own.shape[0]
    for slot in range(SLOTS):
        block = rows[slot * seg : (slot + 1) * seg, :]
        pieces[:, 0, slot * TILE : (slot + 1) * TILE, :] = block.reshape(-1, TILE, DH).astype(BF)
    own[...] = rows[SLOTS * seg :, :].astype(BF)


def pair(block, index):
    return jnp.concatenate(
        [block[:, (2 * index + i) * DH : (2 * index + i + 1) * DH] for i in range(2)], axis=0
    )


def put_pair(block, index, rows):
    seg = block.shape[0]
    for i in range(2):
        block[:, (2 * index + i) * DH : (2 * index + i + 1) * DH] = rows[
            i * seg : (i + 1) * seg, :
        ].astype(BF)


def dot(lhs, rhs, left, right):
    return lax.dot_general(lhs, rhs, (((left,), (right,)), ((), ())), preferred_element_type=F32)


def probs_kernel(table, own, query, grad, key_pieces, key_own, probs, value_pieces, value_own, bias):
    seg = query.shape[0]

    @pl.when(pl.program_id(0) == 0)
    def _():
        key_ids = lax.broadcasted_iota(jnp.int32, (seg, 2 * seg), 0)
        query_ids = lax.broadcasted_iota(jnp.int32, (seg, 2 * seg), 1) % seg
        bias[...] = jnp.where(key_ids <= query_ids, 0.0, -1e30)

    nodes = table.shape[0] // (SLOTS - 1)
    present = [own[0] > 0] + [table[slot * nodes + own[0]] >= 0 for slot in range(SLOTS - 1)]
    levels = [jnp.where(here, 0.0, -1e30).astype(F32) for here in present]
    keys = rows_of(key_pieces, key_own)
    total = jnp.zeros((keys.shape[0], DH), F32)
    for index in range(GROUPS // 2):
        scores = dot(keys, pair(query, index), 1, 1) * (LOG2E / DH**0.5)
        scores = jnp.concatenate(
            [scores[slot * seg : (slot + 1) * seg, :] + levels[slot] for slot in range(SLOTS)]
            + [scores[SLOTS * seg :, :] + bias[...]],
            axis=0,
        )
        weight = jnp.exp2(scores - jnp.max(scores, axis=0, keepdims=True))
        prob = weight * (1.0 / jnp.sum(weight, axis=0, keepdims=True))
        probs[0, :, index * 2 * seg : (index + 1) * 2 * seg] = prob
        total += dot(prob.astype(BF), pair(grad, index), 1, 0)
    put_rows(value_pieces, value_own, total)


def grads_kernel(
    query, grad, probs, key_pieces, key_own, value_pieces, value_own,
    output, query_grad, grad_pieces, grad_own,
):
    seg = query.shape[0]
    keys = rows_of(key_pieces, key_own)
    values = rows_of(value_pieces, value_own)
    keys_t, values_t = keys.T, values.T
    total = jnp.zeros((keys.shape[0], DH), F32)
    for index in range(GROUPS // 2):
        prob = probs[0, :, index * 2 * seg : (index + 1) * 2 * seg]
        dprob = dot(values, pair(grad, index), 1, 1)
        delta = jnp.sum(prob * dprob, axis=0, keepdims=True)
        dscore = (prob * (dprob - delta)).astype(BF)
        total += dot(dscore, pair(query, index), 1, 0)
        put_pair(output, index, dot(values_t, prob.astype(BF), 1, 0).astype(BF).T)
        put_pair(query_grad, index, (dot(keys_t, dscore, 1, 0) * (1.0 / DH**0.5)).astype(BF).T)
    put_rows(grad_pieces, grad_own, total * (1.0 / DH**0.5))


def attention(kernel, lead, arrays, outs, scratch, flops, transcendentals):
    def spec(shape):
        if len(shape) == 4:
            return pl.BlockSpec((shape[0], 1) + shape[2:], lambda h: (0, h, 0, 0))
        if len(shape) == 3:
            return pl.BlockSpec((1,) + shape[1:], lambda h: (h, 0, 0))
        return pl.BlockSpec((shape[0], shape[1] // HK), lambda h: (0, h))

    moved = sum(a.size * a.dtype.itemsize for a in arrays) + sum(
        o.size * o.dtype.itemsize for o in outs
    )
    return pl.pallas_call(
        kernel,
        grid=(HK,),
        out_shape=outs,
        in_specs=[pl.BlockSpec(memory_space=pltpu.SMEM)] * len(lead)
        + [spec(a.shape) for a in arrays],
        out_specs=[spec(o.shape) for o in outs],
        scratch_shapes=scratch,
        compiler_params=pltpu.CompilerParams(vmem_limit_bytes=VMEM_LIMIT),
        cost_estimate=pl.CostEstimate(
            flops=flops, bytes_accessed=moved, transcendentals=transcendentals
        ),
    )(*lead, *arrays)


def project(pieces, own, columns, steps=2):
    blocks = pieces.shape[0]
    seg, width = own.shape
    depth = columns.shape[0]
    return pl.pallas_call(
        project_kernel,
        grid=(steps,),
        out_shape=[
            jax.ShapeDtypeStruct((seg, width), BF),
            jax.ShapeDtypeStruct((depth, width), BF),
        ],
        in_specs=[
            pl.BlockSpec((blocks, HK, TILE, DH), lambda i: (0, 0, SLOTS, 0)),
            pl.BlockSpec((seg, width), lambda i: (0, 0)),
            pl.BlockSpec((depth // steps, seg), lambda i: (i, 0)),
        ],
        out_specs=[
            pl.BlockSpec((seg, width), lambda i: (0, 0)),
            pl.BlockSpec((depth // steps, width), lambda i: (i, 0)),
        ],
        compiler_params=pltpu.CompilerParams(vmem_limit_bytes=VMEM_LIMIT),
        cost_estimate=pl.CostEstimate(
            flops=2 * seg * width * depth,
            bytes_accessed=2 * depth * (width + seg),
            transcendentals=0,
        ),
    )(pieces, own, columns)


def to_pieces(rows):
    seg, width = rows.shape
    split = rows.reshape(seg // TILE, TILE, width // DH, DH).transpose(0, 2, 1, 3)
    return split.reshape(-1, TILE, DH)


def swap(array):
    return lax.all_to_all(array, "leaf", 0, 0, tiled=True)


def shards(n_leaf, n_grp, hidden_states, query_rows, key_rows, value_weight, parent_links, out_grad):
    hidden, query, keys, grad = hidden_states[0], query_rows[0], key_rows[0], out_grad[0]
    seg, width = keys.shape
    depth = hidden.shape[1]
    own_rows = value_weight.shape[0]
    blocks = seg // TILE
    tail = -(-(HK * own_rows + TILE // 2) // TILE) * TILE
    shape = jax.ShapeDtypeStruct
    flops = 2 * seg * 4 * seg * DH * HQ
    select = jnp.asarray(spread_rows(n_leaf, own_rows), BF)
    totals = [pltpu.VMEM((n_leaf, TILE, DH), F32)] * (SLOTS - 1)
    slots = SLOTS * TILE

    columns = hidden.T.reshape(n_leaf, n_grp, own_rows, seg).transpose(1, 0, 2, 3)
    columns = columns.reshape(depth, seg)

    (first,) = plain(
        functools.partial(pack_kernel, own_rows),
        [parent_links, keys, value_weight],
        [shape((n_leaf, TILE + tail, DH), BF)],
        [pltpu.VMEM((tail, DH), F32)],
        scalars=1,
    )
    first = swap(first)

    (weight,) = plain(
        functools.partial(weight_kernel, own_rows),
        [first, select],
        [shape((n_leaf * own_rows, width), BF)],
    )
    weight = lax.all_gather(weight, "grp", axis=0, tiled=True)
    second, table = plain(
        fetch_kernel,
        [first],
        [shape((n_leaf, slots, DH), BF), shape(((SLOTS - 1) * n_leaf,), jnp.int32)],
        [
            pltpu.VMEM((n_leaf, DH), jnp.int32),
            pltpu.SMEM((n_leaf, DH), jnp.int32),
            pltpu.SemaphoreType.DMA,
        ],
        scalar_outs=1,
    )
    key_pieces = swap(second).reshape(blocks, HK, slots, DH)
    probs, value_terms, value_term_own = attention(
        probs_kernel,
        [table, lax.axis_index("leaf").astype(jnp.int32).reshape(1)],
        [query, grad, key_pieces, keys],
        [
            shape((HK, 4 * seg, GROUPS * seg), F32),
            shape((blocks, HK, slots, DH), BF),
            shape((seg, width), BF),
        ],
        [pltpu.VMEM((seg, 2 * seg), F32)],
        2 * flops,
        HQ * seg * 4 * seg,
    )

    values = dot(columns, weight, 0, 0).astype(BF)
    third = jnp.concatenate([value_terms.reshape(-1, slots, DH), to_pieces(values)], axis=1)
    third = swap(third)

    (fourth,) = plain(
        value_kernel, [table, third], [shape((n_leaf, slots + TILE, DH), BF)], totals, scalars=1
    )
    fourth = swap(fourth).reshape(blocks, HK, slots + TILE, DH)
    value_grad, weight_part = project(fourth, value_term_own, columns)
    weight_part = lax.psum_scatter(weight_part, "grp", scatter_dimension=0, tiled=True)
    output, query_grad, key_terms, key_term_own = attention(
        grads_kernel,
        [],
        [query, grad, probs, key_pieces, keys, fourth, values],
        [
            shape((seg, HQ * DH), BF),
            shape((seg, HQ * DH), BF),
            shape((blocks, HK, slots, DH), BF),
            shape((seg, width), BF),
        ],
        [],
        4 * flops,
        0,
    )
    hidden_grad = dot(value_grad, weight, 1, 1).astype(BF)
    hidden_grad = hidden_grad.reshape(seg, n_grp, n_leaf, own_rows).transpose(0, 2, 1, 3)
    hidden_grad = hidden_grad.reshape(seg, depth)

    fifth = swap(key_terms.reshape(-1, slots, DH))

    (key_sums,) = plain(
        key_kernel, [table, fifth], [shape((n_leaf, TILE, DH), BF)], totals, scalars=1
    )
    weight_part, hidden_grad, key_sums = lax.optimization_barrier(
        (weight_part, hidden_grad, key_sums)
    )

    (sixth,) = plain(
        functools.partial(join_kernel, own_rows),
        [key_sums, weight_part, select],
        [shape((n_leaf, TILE + tail, DH), BF)],
    )
    sixth = swap(sixth)
    key_grad, weight_grad = plain(
        functools.partial(last_kernel, own_rows),
        [sixth, key_term_own],
        [shape((seg, width), BF), shape((own_rows, width), F32)],
        [pltpu.VMEM((tail, DH), F32)],
    )
    return (output[None], query_grad[None], key_grad[None], hidden_grad[None], weight_grad)


def solution(mesh):
    rows = P("grp", "leaf", None)
    spread = P(("leaf", "grp"), None)
    return jax.shard_map(
        functools.partial(shards, mesh.shape["leaf"], mesh.shape["grp"]),
        mesh=mesh,
        in_specs=(rows, rows, rows, spread, P("grp", "leaf"), rows),
        out_specs=(rows, rows, rows, rows, spread),
        check_vma=False,
    )
```

```python
import functools

import jax
import jax.numpy as jnp
from jax import lax
from jax.experimental import pallas as pl
from jax.experimental.pallas import tpu as pltpu
from jax.sharding import PartitionSpec as P

HQ = 40
HK = 4
DH = 128
GROUPS = HQ // HK
SLOTS = 3
TILE = 16
LOG2E = 1.4426950408889634
BF = jnp.bfloat16
F32 = jnp.float32
VMEM_LIMIT = 28 * 1024 * 1024
ATTENTION_LIMIT = 56 * 1024 * 1024


def quotient(value, divisor, limit):
    shift = next(
        n
        for n in range(8, 20)
        if all(x * ((1 << n) // divisor + 1) >> n == x // divisor for x in range(limit))
    )
    return (value * ((1 << shift) // divisor + 1)) >> shift


def spread_rows(own_rows):
    count = HK * own_rows
    size = 8 * count
    target = lax.broadcasted_iota(jnp.int32, (size, size), 0)
    leaf = quotient(target, count, size)
    rest = target - leaf * count
    head = quotient(rest, own_rows, count)
    source = (head * 8 + leaf) * own_rows + (rest - head * own_rows)
    found = source == lax.broadcasted_iota(jnp.int32, (size, size), 1)
    return jnp.where(found, 1.0, 0.0).astype(BF)


def pack_kernel(own_rows, parent, keys, weight, sent, rows):
    count = HK * own_rows
    rows[...] = jnp.full(rows.shape, parent[0, 0].astype(F32), F32)
    for head in range(HK):
        rows[head * own_rows : (head + 1) * own_rows, :] = weight[
            :, head * DH : (head + 1) * DH
        ].astype(F32)
    common = rows[...].astype(BF)
    for piece in range(sent.shape[0]):
        block, head = piece // HK, piece % HK
        sent[piece, 0:TILE, :] = keys[block * TILE : (block + 1) * TILE, head * DH : (head + 1) * DH]
        sent[piece, TILE:, :] = common


def weight_kernel(own_rows, held, weight):
    select = spread_rows(own_rows)
    count = HK * own_rows
    for group in range(held.shape[0] // 8):
        part = held[group * 8 : (group + 1) * 8, TILE:, :].astype(F32)[:, :count, :]
        part = part.reshape(8 * count, DH).astype(BF)
        moved = dot(select, part, 0, 0).astype(BF)
        for head in range(HK):
            weight[
                group * 8 * own_rows : (group + 1) * 8 * own_rows, head * DH : (head + 1) * DH
            ] = moved[head * 8 * own_rows : (head + 1) * 8 * own_rows, :]


def fetch_kernel(held, sent, table, wide, parents, arrived):
    nodes = held.shape[0]
    tail = held[:, held.shape[1] - TILE :, :].astype(F32)
    wide[...] = jnp.max(tail[:, TILE // 2 :, :], axis=1).astype(jnp.int32)
    copy = pltpu.make_async_copy(wide, parents, arrived)
    copy.start()
    for node in range(nodes):
        sent[node, 0:TILE, :] = held[0, 0:TILE, :]
    copy.wait()
    for node in range(nodes):
        parent = parents[node, 0]
        above = table[jnp.maximum(parent, 0)] if node > 0 else -1
        deep = jnp.logical_and(parent > 0, above >= 0)
        table[node] = jnp.where(deep, above, jnp.where(parent > 0, parent, -1))
        table[nodes + node] = jnp.where(deep, parent, -1)
    for node in range(nodes):
        for slot in range(1, SLOTS):
            owner = jnp.maximum(table[(slot - 1) * nodes + node], 0)
            sent[node, slot * TILE : (slot + 1) * TILE, :] = held[owner, 0:TILE, :]


def add_up(table, held, totals):
    nodes = held.shape[0]
    for total in totals:
        total[...] = jnp.zeros_like(total)
    root = jnp.zeros((TILE, DH), F32)
    for node in range(nodes):
        root = root + held[node, 0:TILE, :].astype(F32)
        for slot in range(1, SLOTS):
            owner = jnp.maximum(table[(slot - 1) * nodes + node], 0)
            totals[slot - 1][owner] += held[node, slot * TILE : (slot + 1) * TILE, :].astype(F32)
    totals[0][0] += root


def value_kernel(table, held, sent, *totals):
    nodes = held.shape[0]
    values = slice(SLOTS * TILE, (SLOTS + 1) * TILE)
    add_up(table, held, totals)
    for node in range(nodes):
        sent[node, 0:TILE, :] = held[0, values, :]
        for slot in range(1, SLOTS):
            owner = jnp.maximum(table[(slot - 1) * nodes + node], 0)
            sent[node, slot * TILE : (slot + 1) * TILE, :] = held[owner, values, :]
        sent[node, values, :] = (totals[0][node] + totals[1][node]).astype(BF)


def key_kernel(table, held, sums, *totals):
    add_up(table, held, totals)
    for node in range(held.shape[0]):
        sums[node] = (totals[0][node] + totals[1][node]).astype(BF)


def join_kernel(own_rows, sums, part, sent):
    select = spread_rows(own_rows)
    count = HK * own_rows
    sent[:, 0:TILE, :] = sums[...]
    for group in range(sent.shape[0] // 8):
        rows = part[group * 8 * own_rows : (group + 1) * 8 * own_rows, :]
        rows = jnp.concatenate([rows[:, h * DH : (h + 1) * DH] for h in range(HK)], axis=0)
        moved = dot(select, rows, 1, 0).reshape(8, count, DH)
        fill = jnp.zeros((8, sent.shape[1] - TILE - count, DH), F32)
        sent[group * 8 : (group + 1) * 8, TILE:, :] = jnp.concatenate(
            [moved, fill], axis=1
        ).astype(BF)


def last_kernel(own_rows, held, key_own, key_grad, weight_grad, rows):
    for piece in range(held.shape[0]):
        block, head = piece // HK, piece % HK
        at = (slice(block * TILE, (block + 1) * TILE), slice(head * DH, (head + 1) * DH))
        key_grad[at] = (held[piece, 0:TILE, :].astype(F32) + key_own[at].astype(F32)).astype(BF)
    rows[...] = jnp.sum(held[:, TILE:, :].astype(F32), axis=0)
    for head in range(HK):
        weight_grad[:, head * DH : (head + 1) * DH] = rows[
            head * own_rows : (head + 1) * own_rows, :
        ]


def project_kernel(pieces, own, columns, value_grad, part):
    @pl.when(pl.program_id(0) == 0)
    def _():
        for block in range(pieces.shape[0]):
            for head in range(HK):
                at = (slice(block * TILE, (block + 1) * TILE), slice(head * DH, (head + 1) * DH))
                value_grad[at] = (
                    pieces[block, head].astype(F32) + own[at].astype(F32)
                ).astype(BF)

    part[...] = dot(columns[...], value_grad[...], 1, 0).astype(BF)


def plain(kernel, arrays, outs, scratch=(), scalars=0, scalar_outs=0, flops=0):
    smem, vmem = pl.BlockSpec(memory_space=pltpu.SMEM), pl.BlockSpec(memory_space=pltpu.VMEM)
    moved = sum(a.size * a.dtype.itemsize for a in list(arrays) + list(outs))
    return pl.pallas_call(
        kernel,
        out_shape=outs,
        in_specs=[smem] * scalars + [vmem] * (len(arrays) - scalars),
        out_specs=[vmem] * (len(outs) - scalar_outs) + [smem] * scalar_outs,
        scratch_shapes=list(scratch),
        compiler_params=pltpu.CompilerParams(vmem_limit_bytes=VMEM_LIMIT),
        cost_estimate=pl.CostEstimate(flops=flops, bytes_accessed=moved, transcendentals=0),
    )(*arrays)


def rows_of(pieces, own):
    parts = [
        pieces[:, 0, slot * TILE : (slot + 1) * TILE, :].reshape(-1, DH) for slot in range(SLOTS)
    ]
    return jnp.concatenate(parts + [own[...]], axis=0)


def put_rows(pieces, own, rows):
    seg = own.shape[0]
    for slot in range(SLOTS):
        block = rows[slot * seg : (slot + 1) * seg, :]
        pieces[:, 0, slot * TILE : (slot + 1) * TILE, :] = block.reshape(-1, TILE, DH).astype(BF)
    own[...] = rows[SLOTS * seg :, :].astype(BF)


def pair(block, index):
    return jnp.concatenate(
        [block[:, (2 * index + i) * DH : (2 * index + i + 1) * DH] for i in range(2)], axis=0
    )


def heads_of(block):
    return jnp.concatenate([block[:, i * DH : (i + 1) * DH] for i in range(GROUPS)], axis=0)


def put_pair(block, index, rows):
    seg = block.shape[0]
    for i in range(2):
        block[:, (2 * index + i) * DH : (2 * index + i + 1) * DH] = rows[
            i * seg : (i + 1) * seg, :
        ].astype(BF)


def dot(lhs, rhs, left, right):
    return lax.dot_general(lhs, rhs, (((left,), (right,)), ((), ())), preferred_element_type=F32)


def masks_of(table, own, bias):
    seg = bias.shape[0]

    @pl.when(pl.program_id(0) == 0)
    def _():
        key_ids = lax.broadcasted_iota(jnp.int32, bias.shape, 0)
        query_ids = lax.broadcasted_iota(jnp.int32, bias.shape, 1) % seg
        bias[...] = jnp.where(key_ids <= query_ids, 0.0, -1e30)

    nodes = table.shape[0] // (SLOTS - 1)
    present = [own[0] > 0] + [table[slot * nodes + own[0]] >= 0 for slot in range(SLOTS - 1)]
    return [jnp.where(here, 0.0, -1e30).astype(F32) for here in present]


def scores_of(keys, queries, levels, bias):
    seg = bias.shape[0]
    scores = dot(keys, queries, 1, 1) * (LOG2E / DH**0.5)
    return jnp.concatenate(
        [scores[slot * seg : (slot + 1) * seg, :] + levels[slot] for slot in range(SLOTS)]
        + [scores[SLOTS * seg :, :] + bias[...]],
        axis=0,
    )


def probs_kernel(
    table, own, query, grad, key_pieces, key_own, stats, value_pieces, value_own, bias, low
):
    seg = query.shape[0]
    levels = masks_of(table, own, bias)
    keys = rows_of(key_pieces, key_own)
    for index in range(GROUPS // 2):
        at = slice(index * 2 * seg, (index + 1) * 2 * seg)
        scores = scores_of(keys, pair(query, index), levels, bias)
        top = jnp.max(scores, axis=0, keepdims=True)
        weight = jnp.exp2(scores - top)
        norm = 1.0 / jnp.sum(weight, axis=0, keepdims=True)
        stats[0, 0:1, at] = top
        stats[0, 1:2, at] = norm
        low[:, at] = (weight * norm).astype(BF)
    total = dot(low[...], heads_of(grad), 1, 0)
    put_rows(value_pieces, value_own, total)


def grads_kernel(
    table, own, query, grad, stats, key_pieces, key_own, value_pieces, value_own,
    output, query_grad, grad_pieces, grad_own, bias,
):
    seg = query.shape[0]
    levels = masks_of(table, own, bias)
    keys = rows_of(key_pieces, key_own)
    values = rows_of(value_pieces, value_own)
    keys_t, values_t = keys.T, values.T
    total = jnp.zeros((keys.shape[0], DH), F32)
    for index in range(GROUPS // 2):
        at = slice(index * 2 * seg, (index + 1) * 2 * seg)
        queries = pair(query, index)
        scores = scores_of(keys, queries, levels, bias)
        prob = jnp.exp2(scores - stats[0, 0:1, at]) * stats[0, 1:2, at]
        dprob = dot(values, pair(grad, index), 1, 1)
        delta = jnp.sum(prob * dprob, axis=0, keepdims=True)
        dscore = (prob * (dprob - delta)).astype(BF)
        total += dot(dscore, queries, 1, 0)
        put_pair(output, index, dot(values_t, prob.astype(BF), 1, 0).astype(BF).T)
        put_pair(query_grad, index, (dot(keys_t, dscore, 1, 0) * (1.0 / DH**0.5)).astype(BF).T)
    put_rows(grad_pieces, grad_own, total * (1.0 / DH**0.5))


def attention(kernel, lead, arrays, outs, scratch, flops, transcendentals):
    def spec(shape):
        if len(shape) == 4:
            return pl.BlockSpec((shape[0], 1) + shape[2:], lambda h: (0, h, 0, 0))
        if len(shape) == 3:
            return pl.BlockSpec((1,) + shape[1:], lambda h: (h, 0, 0))
        return pl.BlockSpec((shape[0], shape[1] // HK), lambda h: (0, h))

    moved = sum(a.size * a.dtype.itemsize for a in arrays) + sum(
        o.size * o.dtype.itemsize for o in outs
    )
    return pl.pallas_call(
        kernel,
        grid=(HK,),
        out_shape=outs,
        in_specs=[pl.BlockSpec(memory_space=pltpu.SMEM)] * len(lead)
        + [spec(a.shape) for a in arrays],
        out_specs=[spec(o.shape) for o in outs],
        scratch_shapes=scratch,
        compiler_params=pltpu.CompilerParams(vmem_limit_bytes=ATTENTION_LIMIT),
        cost_estimate=pl.CostEstimate(
            flops=flops, bytes_accessed=moved, transcendentals=transcendentals
        ),
    )(*lead, *arrays)


def project(pieces, own, columns, steps=2):
    blocks = pieces.shape[0]
    seg, width = own.shape
    depth = columns.shape[0]
    return pl.pallas_call(
        project_kernel,
        grid=(steps,),
        out_shape=[
            jax.ShapeDtypeStruct((seg, width), BF),
            jax.ShapeDtypeStruct((depth, width), BF),
        ],
        in_specs=[
            pl.BlockSpec((blocks, HK, TILE, DH), lambda i: (0, 0, SLOTS, 0)),
            pl.BlockSpec((seg, width), lambda i: (0, 0)),
            pl.BlockSpec((depth // steps, seg), lambda i: (i, 0)),
        ],
        out_specs=[
            pl.BlockSpec((seg, width), lambda i: (0, 0)),
            pl.BlockSpec((depth // steps, width), lambda i: (i, 0)),
        ],
        compiler_params=pltpu.CompilerParams(vmem_limit_bytes=VMEM_LIMIT),
        cost_estimate=pl.CostEstimate(
            flops=2 * seg * width * depth,
            bytes_accessed=2 * depth * (width + seg),
            transcendentals=0,
        ),
    )(pieces, own, columns)


def to_pieces(rows):
    seg, width = rows.shape
    split = rows.reshape(seg // TILE, TILE, width // DH, DH).transpose(0, 2, 1, 3)
    return split.reshape(-1, TILE, DH)


def swap(array):
    return lax.all_to_all(array, "leaf", 0, 0, tiled=True)


def shards(n_leaf, n_grp, hidden_states, query_rows, key_rows, value_weight, parent_links, out_grad):
    hidden, query, keys, grad = hidden_states[0], query_rows[0], key_rows[0], out_grad[0]
    seg, width = keys.shape
    depth = hidden.shape[1]
    own_rows = value_weight.shape[0]
    blocks = seg // TILE
    tail = -(-(HK * own_rows + TILE // 2) // TILE) * TILE
    shape = jax.ShapeDtypeStruct
    flops = 2 * seg * 4 * seg * DH * HQ
    totals = [pltpu.VMEM((n_leaf, TILE, DH), F32)] * (SLOTS - 1)
    slots = SLOTS * TILE

    columns = hidden.T.reshape(n_leaf, n_grp, own_rows, seg).transpose(1, 0, 2, 3)
    columns = columns.reshape(depth, seg)

    (first,) = plain(
        functools.partial(pack_kernel, own_rows),
        [parent_links, keys, value_weight],
        [shape((n_leaf, TILE + tail, DH), BF)],
        [pltpu.VMEM((tail, DH), F32)],
        scalars=1,
    )
    first = swap(first)

    (weight,) = plain(
        functools.partial(weight_kernel, own_rows),
        [first],
        [shape((n_leaf * own_rows, width), BF)],
    )
    weight = lax.all_gather(weight, "grp", axis=0, tiled=True)
    second, table = plain(
        fetch_kernel,
        [first],
        [shape((n_leaf, slots, DH), BF), shape(((SLOTS - 1) * n_leaf,), jnp.int32)],
        [
            pltpu.VMEM((n_leaf, DH), jnp.int32),
            pltpu.SMEM((n_leaf, DH), jnp.int32),
            pltpu.SemaphoreType.DMA,
        ],
        scalar_outs=1,
    )
    key_pieces = swap(second).reshape(blocks, HK, slots, DH)
    place = [table, lax.axis_index("leaf").astype(jnp.int32).reshape(1)]
    stats, value_terms, value_term_own = attention(
        probs_kernel,
        place,
        [query, grad, key_pieces, keys],
        [
            shape((HK, 8, GROUPS * seg), F32),
            shape((blocks, HK, slots, DH), BF),
            shape((seg, width), BF),
        ],
        [pltpu.VMEM((seg, 2 * seg), F32), pltpu.VMEM((4 * seg, GROUPS * seg), BF)],
        2 * flops,
        HQ * seg * 4 * seg,
    )

    values = dot(columns, weight, 0, 0).astype(BF)
    third = jnp.concatenate([value_terms.reshape(-1, slots, DH), to_pieces(values)], axis=1)
    third = swap(third)

    (fourth,) = plain(
        value_kernel, [table, third], [shape((n_leaf, slots + TILE, DH), BF)], totals, scalars=1
    )
    fourth = swap(fourth).reshape(blocks, HK, slots + TILE, DH)
    value_grad, weight_part = project(fourth, value_term_own, columns)
    weight_part = lax.psum_scatter(weight_part, "grp", scatter_dimension=0, tiled=True)
    output, query_grad, key_terms, key_term_own = attention(
        grads_kernel,
        place,
        [query, grad, stats, key_pieces, keys, fourth, values],
        [
            shape((seg, HQ * DH), BF),
            shape((seg, HQ * DH), BF),
            shape((blocks, HK, slots, DH), BF),
            shape((seg, width), BF),
        ],
        [pltpu.VMEM((seg, 2 * seg), F32)],
        5 * flops,
        HQ * seg * 4 * seg,
    )
    hidden_grad = dot(value_grad, weight, 1, 1).astype(BF)
    hidden_grad = hidden_grad.reshape(seg, n_grp, n_leaf, own_rows).transpose(0, 2, 1, 3)
    hidden_grad = hidden_grad.reshape(seg, depth)

    fifth = swap(key_terms.reshape(-1, slots, DH))

    (key_sums,) = plain(
        key_kernel, [table, fifth], [shape((n_leaf, TILE, DH), BF)], totals, scalars=1
    )
    weight_part, hidden_grad, key_sums = lax.optimization_barrier(
        (weight_part, hidden_grad, key_sums)
    )

    (sixth,) = plain(
        functools.partial(join_kernel, own_rows),
        [key_sums, weight_part],
        [shape((n_leaf, TILE + tail, DH), BF)],
    )
    sixth = swap(sixth)
    key_grad, weight_grad = plain(
        functools.partial(last_kernel, own_rows),
        [sixth, key_term_own],
        [shape((seg, width), BF), shape((own_rows, width), F32)],
        [pltpu.VMEM((tail, DH), F32)],
    )
    return (output[None], query_grad[None], key_grad[None], hidden_grad[None], weight_grad)


def solution(mesh):
    rows = P("grp", "leaf", None)
    spread = P(("leaf", "grp"), None)
    return jax.shard_map(
        functools.partial(shards, mesh.shape["leaf"], mesh.shape["grp"]),
        mesh=mesh,
        in_specs=(rows, rows, rows, spread, P("grp", "leaf"), rows),
        out_specs=(rows, rows, rows, rows, spread),
        check_vma=False,
    )
```

```python
import functools

import jax
import jax.numpy as jnp
from jax import lax
from jax.experimental import pallas as pl
from jax.experimental.layout import Layout, with_layout_constraint
from jax.experimental.pallas import tpu as pltpu
from jax.sharding import PartitionSpec as P

HQ = 40
HK = 4
DH = 128
GROUPS = HQ // HK
SLOTS = 3
TILE = 16
LOG2E = 1.4426950408889634
BF = jnp.bfloat16
F32 = jnp.float32
VMEM_LIMIT = 28 * 1024 * 1024
ATTENTION_LIMIT = 56 * 1024 * 1024


def quotient(value, divisor, limit):
    shift = next(
        n
        for n in range(8, 20)
        if all(x * ((1 << n) // divisor + 1) >> n == x // divisor for x in range(limit))
    )
    return (value * ((1 << shift) // divisor + 1)) >> shift


def spread_rows(own_rows):
    count = HK * own_rows
    size = 8 * count
    target = lax.broadcasted_iota(jnp.int32, (size, size), 0)
    leaf = quotient(target, count, size)
    rest = target - leaf * count
    head = quotient(rest, own_rows, count)
    source = (head * 8 + leaf) * own_rows + (rest - head * own_rows)
    found = source == lax.broadcasted_iota(jnp.int32, (size, size), 1)
    return jnp.where(found, 1.0, 0.0).astype(BF)


def pack_kernel(own_rows, parent, keys, weight, sent, rows):
    count = HK * own_rows
    rows[...] = jnp.full(rows.shape, parent[0, 0].astype(F32), F32)
    for head in range(HK):
        rows[head * own_rows : (head + 1) * own_rows, :] = weight[
            :, head * DH : (head + 1) * DH
        ].astype(F32)
    common = rows[...].astype(BF)
    for piece in range(sent.shape[0]):
        block, head = piece // HK, piece % HK
        sent[piece, 0:TILE, :] = keys[block * TILE : (block + 1) * TILE, head * DH : (head + 1) * DH]
        sent[piece, TILE:, :] = common


def weight_kernel(own_rows, held, weight):
    select = spread_rows(own_rows)
    count = HK * own_rows
    for group in range(held.shape[0] // 8):
        part = held[group * 8 : (group + 1) * 8, TILE:, :].astype(F32)[:, :count, :]
        part = part.reshape(8 * count, DH).astype(BF)
        moved = dot(select, part, 0, 0).astype(BF)
        for head in range(HK):
            weight[
                group * 8 * own_rows : (group + 1) * 8 * own_rows, head * DH : (head + 1) * DH
            ] = moved[head * 8 * own_rows : (head + 1) * 8 * own_rows, :]


def fetch_kernel(held, sent, table, wide, parents, arrived):
    nodes = held.shape[0]
    tail = held[:, held.shape[1] - TILE :, :].astype(F32)
    wide[...] = jnp.max(tail[:, TILE // 2 :, :], axis=1).astype(jnp.int32)
    copy = pltpu.make_async_copy(wide, parents, arrived)
    copy.start()
    for node in range(nodes):
        sent[node, 0:TILE, :] = held[0, 0:TILE, :]
    copy.wait()
    for node in range(nodes):
        parent = parents[node, 0]
        above = table[jnp.maximum(parent, 0)] if node > 0 else -1
        deep = jnp.logical_and(parent > 0, above >= 0)
        table[node] = jnp.where(deep, above, jnp.where(parent > 0, parent, -1))
        table[nodes + node] = jnp.where(deep, parent, -1)
    for node in range(nodes):
        for slot in range(1, SLOTS):
            owner = jnp.maximum(table[(slot - 1) * nodes + node], 0)
            sent[node, slot * TILE : (slot + 1) * TILE, :] = held[owner, 0:TILE, :]


def add_up(table, held, totals):
    nodes = held.shape[0]
    for total in totals:
        total[...] = jnp.zeros_like(total)
    root = jnp.zeros((TILE, DH), F32)
    for node in range(nodes):
        root = root + held[node, 0:TILE, :].astype(F32)
        for slot in range(1, SLOTS):
            owner = jnp.maximum(table[(slot - 1) * nodes + node], 0)
            totals[slot - 1][owner] += held[node, slot * TILE : (slot + 1) * TILE, :].astype(F32)
    totals[0][0] += root


def value_kernel(table, held, sent, *totals):
    nodes = held.shape[0]
    values = slice(SLOTS * TILE, (SLOTS + 1) * TILE)
    add_up(table, held, totals)
    for node in range(nodes):
        sent[node, 0:TILE, :] = held[0, values, :]
        for slot in range(1, SLOTS):
            owner = jnp.maximum(table[(slot - 1) * nodes + node], 0)
            sent[node, slot * TILE : (slot + 1) * TILE, :] = held[owner, values, :]
        sent[node, values, :] = (totals[0][node] + totals[1][node]).astype(BF)


def key_kernel(table, held, sums, *totals):
    add_up(table, held, totals)
    for node in range(held.shape[0]):
        sums[node] = (totals[0][node] + totals[1][node]).astype(BF)


def join_kernel(own_rows, sums, part, sent):
    select = spread_rows(own_rows)
    count = HK * own_rows
    sent[:, 0:TILE, :] = sums[...]
    for group in range(sent.shape[0] // 8):
        rows = part[group * 8 * own_rows : (group + 1) * 8 * own_rows, :]
        rows = jnp.concatenate([rows[:, h * DH : (h + 1) * DH] for h in range(HK)], axis=0)
        moved = dot(select, rows, 1, 0).reshape(8, count, DH)
        fill = jnp.zeros((8, sent.shape[1] - TILE - count, DH), F32)
        sent[group * 8 : (group + 1) * 8, TILE:, :] = jnp.concatenate(
            [moved, fill], axis=1
        ).astype(BF)


def last_kernel(own_rows, held, key_own, key_grad, weight_grad, rows):
    for piece in range(held.shape[0]):
        block, head = piece // HK, piece % HK
        at = (slice(block * TILE, (block + 1) * TILE), slice(head * DH, (head + 1) * DH))
        key_grad[at] = (held[piece, 0:TILE, :].astype(F32) + key_own[at].astype(F32)).astype(BF)
    rows[...] = jnp.sum(held[:, TILE:, :].astype(F32), axis=0)
    for head in range(HK):
        weight_grad[:, head * DH : (head + 1) * DH] = rows[
            head * own_rows : (head + 1) * own_rows, :
        ]


def project_kernel(pieces, own, columns, value_grad, part):
    @pl.when(pl.program_id(0) == 0)
    def _():
        for block in range(pieces.shape[0]):
            for head in range(HK):
                at = (slice(block * TILE, (block + 1) * TILE), slice(head * DH, (head + 1) * DH))
                value_grad[at] = (
                    pieces[block, head].astype(F32) + own[at].astype(F32)
                ).astype(BF)

    part[...] = dot(columns[...], value_grad[...], 1, 0).astype(BF)


def plain(kernel, arrays, outs, scratch=(), scalars=0, scalar_outs=0, flops=0):
    smem, vmem = pl.BlockSpec(memory_space=pltpu.SMEM), pl.BlockSpec(memory_space=pltpu.VMEM)
    moved = sum(a.size * a.dtype.itemsize for a in list(arrays) + list(outs))
    return pl.pallas_call(
        kernel,
        out_shape=outs,
        in_specs=[smem] * scalars + [vmem] * (len(arrays) - scalars),
        out_specs=[vmem] * (len(outs) - scalar_outs) + [smem] * scalar_outs,
        scratch_shapes=list(scratch),
        compiler_params=pltpu.CompilerParams(vmem_limit_bytes=VMEM_LIMIT),
        cost_estimate=pl.CostEstimate(flops=flops, bytes_accessed=moved, transcendentals=0),
    )(*arrays)


def rows_of(pieces, own):
    parts = [
        pieces[:, 0, slot * TILE : (slot + 1) * TILE, :].reshape(-1, DH) for slot in range(SLOTS)
    ]
    return jnp.concatenate(parts + [own[...]], axis=0)


def put_rows(pieces, own, rows):
    seg = own.shape[0]
    for slot in range(SLOTS):
        block = rows[slot * seg : (slot + 1) * seg, :]
        pieces[:, 0, slot * TILE : (slot + 1) * TILE, :] = block.reshape(-1, TILE, DH).astype(BF)
    own[...] = rows[SLOTS * seg :, :].astype(BF)


def pair(block, index):
    return jnp.concatenate(
        [block[:, (2 * index + i) * DH : (2 * index + i + 1) * DH] for i in range(2)], axis=0
    )


def heads_of(block):
    return jnp.concatenate([block[:, i * DH : (i + 1) * DH] for i in range(GROUPS)], axis=0)


def put_pair(block, index, rows):
    seg = block.shape[0]
    for i in range(2):
        block[:, (2 * index + i) * DH : (2 * index + i + 1) * DH] = rows[
            i * seg : (i + 1) * seg, :
        ].astype(BF)


def dot(lhs, rhs, left, right):
    return lax.dot_general(lhs, rhs, (((left,), (right,)), ((), ())), preferred_element_type=F32)


def masks_of(present, bias):
    seg = bias.shape[0]

    @pl.when(pl.program_id(0) == 0)
    def _():
        key_ids = lax.broadcasted_iota(jnp.int32, bias.shape, 0)
        query_ids = lax.broadcasted_iota(jnp.int32, bias.shape, 1) % seg
        bias[...] = jnp.where(key_ids <= query_ids, 0.0, -1e30)

    return [jnp.where(present[slot] > 0, 0.0, -1e30).astype(F32) for slot in range(SLOTS)]


def scores_of(keys, queries, levels, bias):
    seg = bias.shape[0]
    scores = dot(keys, queries, 1, 1) * (LOG2E / DH**0.5)
    return jnp.concatenate(
        [scores[slot * seg : (slot + 1) * seg, :] + levels[slot] for slot in range(SLOTS)]
        + [scores[SLOTS * seg :, :] + bias[...]],
        axis=0,
    )


def probs_kernel(
    present, query, grad, key_pieces, key_own, stats, value_pieces, value_own, bias, low
):
    seg = query.shape[0]
    levels = masks_of(present, bias)
    keys = rows_of(key_pieces, key_own)
    for index in range(GROUPS // 2):
        at = slice(index * 2 * seg, (index + 1) * 2 * seg)
        scores = scores_of(keys, pair(query, index), levels, bias)
        top = jnp.max(scores, axis=0, keepdims=True)
        weight = jnp.exp2(scores - top)
        norm = 1.0 / jnp.sum(weight, axis=0, keepdims=True)
        stats[0, 0:1, at] = top
        stats[0, 1:2, at] = norm
        low[:, at] = (weight * norm).astype(BF)
    total = dot(low[...], heads_of(grad), 1, 0)
    put_rows(value_pieces, value_own, total)


def grads_kernel(
    present, query, grad, stats, key_pieces, key_own, value_pieces, value_own,
    output, query_grad, grad_pieces, grad_own, bias,
):
    seg = query.shape[0]
    levels = masks_of(present, bias)
    keys = rows_of(key_pieces, key_own)
    values = rows_of(value_pieces, value_own)
    keys_t, values_t = keys.T, values.T
    total = jnp.zeros((keys.shape[0], DH), F32)
    for index in range(GROUPS // 2):
        at = slice(index * 2 * seg, (index + 1) * 2 * seg)
        queries = pair(query, index)
        scores = scores_of(keys, queries, levels, bias)
        prob = jnp.exp2(scores - stats[0, 0:1, at]) * stats[0, 1:2, at]
        dprob = dot(values, pair(grad, index), 1, 1)
        delta = jnp.sum(prob * dprob, axis=0, keepdims=True)
        dscore = (prob * (dprob - delta)).astype(BF)
        total += dot(dscore, queries, 1, 0)
        put_pair(output, index, dot(values_t, prob.astype(BF), 1, 0).astype(BF).T)
        put_pair(query_grad, index, (dot(keys_t, dscore, 1, 0) * (1.0 / DH**0.5)).astype(BF).T)
    put_rows(grad_pieces, grad_own, total * (1.0 / DH**0.5))


def attention(kernel, lead, arrays, outs, scratch, flops, transcendentals):
    def spec(shape):
        if len(shape) == 4:
            return pl.BlockSpec((shape[0], 1) + shape[2:], lambda h: (0, h, 0, 0))
        if len(shape) == 3:
            return pl.BlockSpec((1,) + shape[1:], lambda h: (h, 0, 0))
        return pl.BlockSpec((shape[0], shape[1] // HK), lambda h: (0, h))

    moved = sum(a.size * a.dtype.itemsize for a in arrays) + sum(
        o.size * o.dtype.itemsize for o in outs
    )
    return pl.pallas_call(
        kernel,
        grid=(HK,),
        out_shape=outs,
        in_specs=[pl.BlockSpec(memory_space=pltpu.SMEM)] * len(lead)
        + [spec(a.shape) for a in arrays],
        out_specs=[spec(o.shape) for o in outs],
        scratch_shapes=scratch,
        compiler_params=pltpu.CompilerParams(vmem_limit_bytes=ATTENTION_LIMIT),
        cost_estimate=pl.CostEstimate(
            flops=flops, bytes_accessed=moved, transcendentals=transcendentals
        ),
    )(*lead, *arrays)


def project(pieces, own, columns, steps=2):
    blocks = pieces.shape[0]
    seg, width = own.shape
    depth = columns.shape[0]
    return pl.pallas_call(
        project_kernel,
        grid=(steps,),
        out_shape=[
            jax.ShapeDtypeStruct((seg, width), BF),
            jax.ShapeDtypeStruct((depth, width), BF),
        ],
        in_specs=[
            pl.BlockSpec((blocks, HK, TILE, DH), lambda i: (0, 0, SLOTS, 0)),
            pl.BlockSpec((seg, width), lambda i: (0, 0)),
            pl.BlockSpec((depth // steps, seg), lambda i: (i, 0)),
        ],
        out_specs=[
            pl.BlockSpec((seg, width), lambda i: (0, 0)),
            pl.BlockSpec((depth // steps, width), lambda i: (i, 0)),
        ],
        compiler_params=pltpu.CompilerParams(vmem_limit_bytes=VMEM_LIMIT),
        cost_estimate=pl.CostEstimate(
            flops=2 * seg * width * depth,
            bytes_accessed=2 * depth * (width + seg),
            transcendentals=0,
        ),
    )(pieces, own, columns)


def to_pieces(rows):
    seg, width = rows.shape
    split = rows.reshape(seg // TILE, TILE, width // DH, DH).transpose(0, 2, 1, 3)
    return split.reshape(-1, TILE, DH)


def swap(array):
    return lax.all_to_all(array, "leaf", 0, 0, tiled=True)


def shards(n_leaf, n_grp, hidden_states, query_rows, key_rows, value_weight, parent_links, out_grad):
    hidden, query, keys, grad = hidden_states[0], query_rows[0], key_rows[0], out_grad[0]
    seg, width = keys.shape
    depth = hidden.shape[1]
    own_rows = value_weight.shape[0]
    blocks = seg // TILE
    tail = -(-(HK * own_rows + TILE // 2) // TILE) * TILE
    shape = jax.ShapeDtypeStruct
    flops = 2 * seg * 4 * seg * DH * HQ
    totals = [pltpu.VMEM((n_leaf, TILE, DH), F32)] * (SLOTS - 1)
    slots = SLOTS * TILE

    columns = hidden.T.reshape(n_leaf, n_grp, own_rows, seg).transpose(1, 0, 2, 3)
    columns = columns.reshape(depth, seg)

    (first,) = plain(
        functools.partial(pack_kernel, own_rows),
        [parent_links, keys, value_weight],
        [shape((n_leaf, TILE + tail, DH), BF)],
        [pltpu.VMEM((tail, DH), F32)],
        scalars=1,
    )
    first = swap(first)

    (weight,) = plain(
        functools.partial(weight_kernel, own_rows),
        [first],
        [shape((n_leaf * own_rows, width), BF)],
    )
    weight = lax.all_gather(weight, "grp", axis=0, tiled=True)
    second, table = plain(
        fetch_kernel,
        [first],
        [shape((n_leaf, slots, DH), BF), shape(((SLOTS - 1) * n_leaf,), jnp.int32)],
        [
            pltpu.VMEM((n_leaf, DH), jnp.int32),
            pltpu.SMEM((n_leaf, DH), jnp.int32),
            pltpu.SemaphoreType.DMA,
        ],
        scalar_outs=1,
    )
    key_pieces = swap(second).reshape(blocks, HK, slots, DH)
    own = lax.axis_index("leaf")
    here = (table.reshape(SLOTS - 1, n_leaf) >= 0) & (jnp.arange(n_leaf) == own)
    present = jnp.concatenate([(own > 0)[None], jnp.any(here, axis=1)]).astype(jnp.int32)
    stats, value_terms, value_term_own = attention(
        probs_kernel,
        [present],
        [query, grad, key_pieces, keys],
        [
            shape((HK, 8, GROUPS * seg), F32),
            shape((blocks, HK, slots, DH), BF),
            shape((seg, width), BF),
        ],
        [pltpu.VMEM((seg, 2 * seg), F32), pltpu.VMEM((4 * seg, GROUPS * seg), BF)],
        2 * flops,
        HQ * seg * 4 * seg,
    )

    values = dot(columns, weight, 0, 0).astype(BF)
    third = jnp.concatenate([value_terms.reshape(-1, slots, DH), to_pieces(values)], axis=1)
    third = swap(third)

    (fourth,) = plain(
        value_kernel, [table, third], [shape((n_leaf, slots + TILE, DH), BF)], totals, scalars=1
    )
    fourth = swap(fourth).reshape(blocks, HK, slots + TILE, DH)
    value_grad, weight_part = project(fourth, value_term_own, columns)
    weight_part = lax.psum_scatter(weight_part, "grp", scatter_dimension=0, tiled=True)
    output, query_grad, key_terms, key_term_own = attention(
        grads_kernel,
        [present],
        [query, grad, stats, key_pieces, keys, fourth, values],
        [
            shape((seg, HQ * DH), BF),
            shape((seg, HQ * DH), BF),
            shape((blocks, HK, slots, DH), BF),
            shape((seg, width), BF),
        ],
        [pltpu.VMEM((seg, 2 * seg), F32)],
        5 * flops,
        HQ * seg * 4 * seg,
    )
    hidden_grad = dot(value_grad, weight, 1, 1).astype(BF)
    hidden_grad = hidden_grad.reshape(seg, n_grp, n_leaf, own_rows).transpose(0, 2, 1, 3)
    hidden_grad = with_layout_constraint(
        hidden_grad.reshape(1, seg, depth), Layout(major_to_minor=(0, 1, 2))
    )

    fifth = swap(key_terms.reshape(-1, slots, DH))

    (key_sums,) = plain(
        key_kernel, [table, fifth], [shape((n_leaf, TILE, DH), BF)], totals, scalars=1
    )
    weight_part, hidden_grad, key_sums = lax.optimization_barrier(
        (weight_part, hidden_grad, key_sums)
    )

    (sixth,) = plain(
        functools.partial(join_kernel, own_rows),
        [key_sums, weight_part],
        [shape((n_leaf, TILE + tail, DH), BF)],
    )
    sixth = swap(sixth)
    key_grad, weight_grad = plain(
        functools.partial(last_kernel, own_rows),
        [sixth, key_term_own],
        [shape((seg, width), BF), shape((own_rows, width), F32)],
        [pltpu.VMEM((tail, DH), F32)],
    )
    return (output[None], query_grad[None], key_grad[None], hidden_grad, weight_grad)


def solution(mesh):
    rows = P("grp", "leaf", None)
    spread = P(("leaf", "grp"), None)
    return jax.shard_map(
        functools.partial(shards, mesh.shape["leaf"], mesh.shape["grp"]),
        mesh=mesh,
        in_specs=(rows, rows, rows, spread, P("grp", "leaf"), rows),
        out_specs=(rows, rows, rows, rows, spread),
        check_vma=False,
    )
```

```python
import functools

import jax
import jax.numpy as jnp
from jax import lax
from jax.experimental import pallas as pl
from jax.experimental.layout import Layout, with_layout_constraint
from jax.experimental.pallas import tpu as pltpu
from jax.sharding import PartitionSpec as P

HQ = 40
HK = 4
DH = 128
GROUPS = HQ // HK
SLOTS = 3
TILE = 16
LOG2E = 1.4426950408889634
BF = jnp.bfloat16
F32 = jnp.float32
VMEM_LIMIT = 28 * 1024 * 1024
ATTENTION_LIMIT = 56 * 1024 * 1024


def quotient(value, divisor, limit):
    shift = next(
        n
        for n in range(8, 20)
        if all(x * ((1 << n) // divisor + 1) >> n == x // divisor for x in range(limit))
    )
    return (value * ((1 << shift) // divisor + 1)) >> shift


def spread_rows(own_rows):
    count = HK * own_rows
    size = 8 * count
    target = lax.broadcasted_iota(jnp.int32, (size, size), 0)
    leaf = quotient(target, count, size)
    rest = target - leaf * count
    head = quotient(rest, own_rows, count)
    source = (head * 8 + leaf) * own_rows + (rest - head * own_rows)
    found = source == lax.broadcasted_iota(jnp.int32, (size, size), 1)
    return jnp.where(found, 1.0, 0.0).astype(BF)


def pack_kernel(own_rows, parent, keys, weight, sent, rows):
    count = HK * own_rows
    rows[...] = jnp.broadcast_to(parent[...].astype(F32), rows.shape)
    for head in range(HK):
        rows[head * own_rows : (head + 1) * own_rows, :] = weight[
            :, head * DH : (head + 1) * DH
        ].astype(F32)
    common = rows[...].astype(BF)
    for piece in range(sent.shape[0]):
        block, head = piece // HK, piece % HK
        sent[piece, 0:TILE, :] = keys[block * TILE : (block + 1) * TILE, head * DH : (head + 1) * DH]
        sent[piece, TILE:, :] = common


def weight_kernel(own_rows, held, weight):
    select = spread_rows(own_rows)
    count = HK * own_rows
    for group in range(held.shape[0] // 8):
        part = held[group * 8 : (group + 1) * 8, TILE:, :].astype(F32)[:, :count, :]
        part = part.reshape(8 * count, DH).astype(BF)
        moved = dot(select, part, 0, 0).astype(BF)
        for head in range(HK):
            weight[
                group * 8 * own_rows : (group + 1) * 8 * own_rows, head * DH : (head + 1) * DH
            ] = moved[head * 8 * own_rows : (head + 1) * 8 * own_rows, :]


def fetch_kernel(held, sent, table, wide, parents, arrived):
    nodes = held.shape[0]
    tail = held[:, held.shape[1] - TILE :, :].astype(F32)
    wide[...] = jnp.max(tail[:, TILE // 2 :, :], axis=1).astype(jnp.int32)
    copy = pltpu.make_async_copy(wide, parents, arrived)
    copy.start()
    for node in range(nodes):
        sent[node, 0:TILE, :] = held[0, 0:TILE, :]
    copy.wait()
    for node in range(nodes):
        parent = parents[node, 0]
        above = table[jnp.maximum(parent, 0)] if node > 0 else -1
        deep = jnp.logical_and(parent > 0, above >= 0)
        table[node] = jnp.where(deep, above, jnp.where(parent > 0, parent, -1))
        table[nodes + node] = jnp.where(deep, parent, -1)
    for node in range(nodes):
        for slot in range(1, SLOTS):
            owner = jnp.maximum(table[(slot - 1) * nodes + node], 0)
            sent[node, slot * TILE : (slot + 1) * TILE, :] = held[owner, 0:TILE, :]


def add_up(table, held, totals):
    nodes = held.shape[0]
    for total in totals:
        total[...] = jnp.zeros_like(total)
    root = jnp.zeros((TILE, DH), F32)
    for node in range(nodes):
        root = root + held[node, 0:TILE, :].astype(F32)
        for slot in range(1, SLOTS):
            owner = jnp.maximum(table[(slot - 1) * nodes + node], 0)
            totals[slot - 1][owner] += held[node, slot * TILE : (slot + 1) * TILE, :].astype(F32)
    totals[0][0] += root


def value_kernel(table, held, sent, *totals):
    nodes = held.shape[0]
    values = slice(SLOTS * TILE, (SLOTS + 1) * TILE)
    add_up(table, held, totals)
    for node in range(nodes):
        sent[node, 0:TILE, :] = held[0, values, :]
        for slot in range(1, SLOTS):
            owner = jnp.maximum(table[(slot - 1) * nodes + node], 0)
            sent[node, slot * TILE : (slot + 1) * TILE, :] = held[owner, values, :]
        sent[node, values, :] = (totals[0][node] + totals[1][node]).astype(BF)


def key_kernel(table, held, sums, *totals):
    add_up(table, held, totals)
    for node in range(held.shape[0]):
        sums[node] = (totals[0][node] + totals[1][node]).astype(BF)


def join_kernel(own_rows, sums, part, sent):
    select = spread_rows(own_rows)
    count = HK * own_rows
    sent[:, 0:TILE, :] = sums[...]
    for group in range(sent.shape[0] // 8):
        rows = part[group * 8 * own_rows : (group + 1) * 8 * own_rows, :]
        rows = jnp.concatenate([rows[:, h * DH : (h + 1) * DH] for h in range(HK)], axis=0)
        moved = dot(select, rows, 1, 0).reshape(8, count, DH)
        fill = jnp.zeros((8, sent.shape[1] - TILE - count, DH), F32)
        sent[group * 8 : (group + 1) * 8, TILE:, :] = jnp.concatenate(
            [moved, fill], axis=1
        ).astype(BF)


def last_kernel(own_rows, held, key_own, key_grad, weight_grad, rows):
    for piece in range(held.shape[0]):
        block, head = piece // HK, piece % HK
        at = (slice(block * TILE, (block + 1) * TILE), slice(head * DH, (head + 1) * DH))
        key_grad[at] = (held[piece, 0:TILE, :].astype(F32) + key_own[at].astype(F32)).astype(BF)
    rows[...] = jnp.sum(held[:, TILE:, :].astype(F32), axis=0)
    for head in range(HK):
        weight_grad[:, head * DH : (head + 1) * DH] = rows[
            head * own_rows : (head + 1) * own_rows, :
        ]


def plain(kernel, arrays, outs, scratch=(), scalars=0, scalar_outs=0, limit=VMEM_LIMIT):
    smem, vmem = pl.BlockSpec(memory_space=pltpu.SMEM), pl.BlockSpec(memory_space=pltpu.VMEM)
    moved = sum(a.size * a.dtype.itemsize for a in list(arrays) + list(outs))
    return pl.pallas_call(
        kernel,
        out_shape=outs,
        in_specs=[smem] * scalars + [vmem] * (len(arrays) - scalars),
        out_specs=[vmem] * (len(outs) - scalar_outs) + [smem] * scalar_outs,
        scratch_shapes=list(scratch),
        compiler_params=pltpu.CompilerParams(vmem_limit_bytes=limit),
        cost_estimate=pl.CostEstimate(flops=0, bytes_accessed=moved, transcendentals=0),
    )(*arrays)


def rows_of(pieces, own):
    parts = [
        pieces[:, 0, slot * TILE : (slot + 1) * TILE, :].reshape(-1, DH) for slot in range(SLOTS)
    ]
    return jnp.concatenate(parts + [own[...]], axis=0)


def put_rows(pieces, own, rows):
    seg = own.shape[0]
    for slot in range(SLOTS):
        block = rows[slot * seg : (slot + 1) * seg, :]
        pieces[:, 0, slot * TILE : (slot + 1) * TILE, :] = block.reshape(-1, TILE, DH).astype(BF)
    own[...] = rows[SLOTS * seg :, :].astype(BF)


def pair(block, index):
    return jnp.concatenate(
        [block[:, (2 * index + i) * DH : (2 * index + i + 1) * DH] for i in range(2)], axis=0
    )


def heads_of(block):
    return jnp.concatenate([block[:, i * DH : (i + 1) * DH] for i in range(GROUPS)], axis=0)


def put_pair(block, index, rows):
    seg = block.shape[0]
    for i in range(2):
        block[:, (2 * index + i) * DH : (2 * index + i + 1) * DH] = rows[
            i * seg : (i + 1) * seg, :
        ].astype(BF)


def dot(lhs, rhs, left, right):
    return lax.dot_general(lhs, rhs, (((left,), (right,)), ((), ())), preferred_element_type=F32)


def masks_of(present, bias):
    seg = bias.shape[0]

    @pl.when(pl.program_id(0) == 0)
    def _():
        key_ids = lax.broadcasted_iota(jnp.int32, bias.shape, 0)
        query_ids = lax.broadcasted_iota(jnp.int32, bias.shape, 1) % seg
        bias[...] = jnp.where(key_ids <= query_ids, 0.0, -1e30)

    return [jnp.where(present[slot] > 0, 0.0, -1e30).astype(F32) for slot in range(SLOTS)]


def scores_of(keys, queries, levels, bias):
    seg = bias.shape[0]
    scores = dot(keys, queries, 1, 1) * (LOG2E / DH**0.5)
    return jnp.concatenate(
        [scores[slot * seg : (slot + 1) * seg, :] + levels[slot] for slot in range(SLOTS)]
        + [scores[SLOTS * seg :, :] + bias[...]],
        axis=0,
    )


def probs_kernel(
    present, query, grad, key_pieces, key_own, probs, value_pieces, value_own, bias, low
):
    seg = query.shape[0]
    levels = masks_of(present, bias)
    keys = rows_of(key_pieces, key_own)
    for index in range(GROUPS // 2):
        at = slice(index * 2 * seg, (index + 1) * 2 * seg)
        scores = scores_of(keys, pair(query, index), levels, bias)
        weight = jnp.exp2(scores - jnp.max(scores, axis=0, keepdims=True))
        prob = weight * (1.0 / jnp.sum(weight, axis=0, keepdims=True))
        probs[0, :, at] = prob
        low[:, at] = prob.astype(BF)
    put_rows(value_pieces, value_own, dot(low[...], heads_of(grad), 1, 0))


def grads_kernel(
    query, grad, probs, key_pieces, key_own, value_pieces, value_own,
    output, query_grad, grad_pieces, grad_own, low,
):
    seg = query.shape[0]
    keys = rows_of(key_pieces, key_own)
    values = rows_of(value_pieces, value_own)
    keys_t, values_t = keys.T, values.T
    for index in range(GROUPS // 2):
        at = slice(index * 2 * seg, (index + 1) * 2 * seg)
        prob = probs[0, :, at]
        dprob = dot(values, pair(grad, index), 1, 1)
        delta = jnp.sum(prob * dprob, axis=0, keepdims=True)
        dscore = (prob * (dprob - delta)).astype(BF)
        low[:, at] = dscore
        put_pair(output, index, dot(values_t, prob.astype(BF), 1, 0).astype(BF).T)
        put_pair(query_grad, index, (dot(keys_t, dscore, 1, 0) * (1.0 / DH**0.5)).astype(BF).T)
    total = dot(low[...], heads_of(query), 1, 0)
    put_rows(grad_pieces, grad_own, total * (1.0 / DH**0.5))


def attention(kernel, lead, arrays, outs, scratch, flops, transcendentals):
    def spec(shape):
        if len(shape) == 4:
            return pl.BlockSpec((shape[0], 1) + shape[2:], lambda h: (0, h, 0, 0))
        if len(shape) == 3:
            return pl.BlockSpec((1,) + shape[1:], lambda h: (h, 0, 0))
        return pl.BlockSpec((shape[0], shape[1] // HK), lambda h: (0, h))

    moved = sum(a.size * a.dtype.itemsize for a in arrays) + sum(
        o.size * o.dtype.itemsize for o in outs
    )
    return pl.pallas_call(
        kernel,
        grid=(HK,),
        out_shape=outs,
        in_specs=[pl.BlockSpec(memory_space=pltpu.SMEM)] * len(lead)
        + [spec(a.shape) for a in arrays],
        out_specs=[spec(o.shape) for o in outs],
        scratch_shapes=scratch,
        compiler_params=pltpu.CompilerParams(vmem_limit_bytes=ATTENTION_LIMIT),
        cost_estimate=pl.CostEstimate(
            flops=flops, bytes_accessed=moved, transcendentals=transcendentals
        ),
    )(*lead, *arrays)


def share_kernel(which, pieces, own, columns, value_grad, part):
    @pl.when(pl.program_id(0) == 0)
    def _():
        for block in range(pieces.shape[0]):
            for head in range(HK):
                at = (slice(block * TILE, (block + 1) * TILE), slice(head * DH, (head + 1) * DH))
                value_grad[at] = (
                    pieces[block, head].astype(F32) + own[at].astype(F32)
                ).astype(BF)

    part[...] = dot(columns[...], value_grad[...], 1, 0).astype(BF)


def combine_kernel(which, value_grad, columns, arrived, part):
    own = dot(columns[...], value_grad[...], 1, 0)
    part[...] = (own + arrived[...].astype(F32)).astype(BF)


def share(kernel, which, first, columns, rest, outs, n_grp):
    rows = columns.shape[0] // n_grp

    def spec(shape):
        if len(shape) == 4:
            return pl.BlockSpec(shape[:2] + (TILE, DH), lambda i, which: (0, 0, SLOTS, 0))
        if shape[0] == columns.shape[1]:
            return pl.BlockSpec(shape, lambda i, which: (0, 0))
        return pl.BlockSpec((rows, shape[1]), lambda i, which: (i, 0))

    return pl.pallas_call(
        kernel,
        out_shape=outs,
        grid_spec=pltpu.PrefetchScalarGridSpec(
            num_scalar_prefetch=1,
            grid=(n_grp // 2,),
            in_specs=[spec(a.shape) for a in first]
            + [pl.BlockSpec((rows, columns.shape[1]), lambda i, which: (2 * i + which[0], 0))]
            + [spec(a.shape) for a in rest],
            out_specs=[spec(o.shape) for o in outs],
        ),
        compiler_params=pltpu.CompilerParams(vmem_limit_bytes=VMEM_LIMIT),
        cost_estimate=pl.CostEstimate(
            flops=columns.size * 512, bytes_accessed=columns.size * 5, transcendentals=0
        ),
    )(which, *first, columns, *rest)


def to_pieces(rows):
    seg, width = rows.shape
    split = rows.reshape(seg // TILE, TILE, width // DH, DH).transpose(0, 2, 1, 3)
    return split.reshape(-1, TILE, DH)


def swap(array):
    return lax.all_to_all(array, "leaf", 0, 0, tiled=True)


def shards(n_leaf, n_grp, hidden_states, query_rows, key_rows, value_weight, parent_links, out_grad):
    hidden, query, keys, grad = hidden_states[0], query_rows[0], key_rows[0], out_grad[0]
    seg, width = keys.shape
    depth = hidden.shape[1]
    own_rows = value_weight.shape[0]
    blocks = seg // TILE
    tail = -(-(HK * own_rows + TILE // 2) // TILE) * TILE
    shape = jax.ShapeDtypeStruct
    flops = 2 * seg * 4 * seg * DH * HQ
    totals = [pltpu.VMEM((n_leaf, TILE, DH), F32)] * (SLOTS - 1)
    slots = SLOTS * TILE

    columns = hidden.T.reshape(n_leaf, n_grp, own_rows, seg).transpose(1, 0, 2, 3)
    columns = columns.reshape(depth, seg)
    core = lax.axis_index("grp").astype(jnp.int32).reshape(1) % 2

    (first,) = plain(
        functools.partial(pack_kernel, own_rows),
        [parent_links, keys, value_weight],
        [shape((n_leaf, TILE + tail, DH), BF)],
        [pltpu.VMEM((tail, DH), F32)],
        limit=ATTENTION_LIMIT,
    )
    first = swap(first)

    (weight,) = plain(
        functools.partial(weight_kernel, own_rows),
        [first],
        [shape((n_leaf * own_rows, width), BF)],
    )
    weight = lax.all_gather(weight, "grp", axis=0, tiled=True)
    second, table = plain(
        fetch_kernel,
        [first],
        [shape((n_leaf, slots, DH), BF), shape(((SLOTS - 1) * n_leaf,), jnp.int32)],
        [
            pltpu.VMEM((n_leaf, DH), jnp.int32),
            pltpu.SMEM((n_leaf, DH), jnp.int32),
            pltpu.SemaphoreType.DMA,
        ],
        scalar_outs=1,
    )
    key_pieces = swap(second).reshape(blocks, HK, slots, DH)
    own = lax.axis_index("leaf")
    here = (table.reshape(SLOTS - 1, n_leaf) >= 0) & (jnp.arange(n_leaf) == own)
    present = jnp.concatenate([(own > 0)[None], jnp.any(here, axis=1)]).astype(jnp.int32)
    probs, value_terms, value_term_own = attention(
        probs_kernel,
        [present],
        [query, grad, key_pieces, keys],
        [
            shape((HK, 4 * seg, GROUPS * seg), F32),
            shape((blocks, HK, slots, DH), BF),
            shape((seg, width), BF),
        ],
        [pltpu.VMEM((seg, 2 * seg), F32), pltpu.VMEM((4 * seg, GROUPS * seg), BF)],
        2 * flops,
        HQ * seg * 4 * seg,
    )

    values = dot(columns, weight, 0, 0).astype(BF)
    third = jnp.concatenate([value_terms.reshape(-1, slots, DH), to_pieces(values)], axis=1)
    third = swap(third)

    (fourth,) = plain(
        value_kernel, [table, third], [shape((n_leaf, slots + TILE, DH), BF)], totals, scalars=1
    )
    fourth = swap(fourth).reshape(blocks, HK, slots + TILE, DH)
    half = shape((depth // 2, width), BF)
    value_grad, weight_part = share(
        share_kernel,
        1 - core,
        [fourth, value_term_own],
        columns,
        [],
        [shape((seg, width), BF), half],
        n_grp,
    )
    weight_part = lax.ppermute(weight_part, "grp", [(i, i ^ 1) for i in range(n_grp)])
    (weight_part,) = share(
        combine_kernel, core, [value_grad], columns, [weight_part], [half], n_grp
    )
    weight_part = lax.psum_scatter(
        weight_part,
        "grp",
        scatter_dimension=0,
        axis_index_groups=[list(range(c, n_grp, 2)) for c in range(2)],
        tiled=True,
    )
    output, query_grad, key_terms, key_term_own = attention(
        grads_kernel,
        [],
        [query, grad, probs, key_pieces, keys, fourth, values],
        [
            shape((seg, HQ * DH), BF),
            shape((seg, HQ * DH), BF),
            shape((blocks, HK, slots, DH), BF),
            shape((seg, width), BF),
        ],
        [pltpu.VMEM((4 * seg, GROUPS * seg), BF)],
        4 * flops,
        0,
    )
    hidden_grad = dot(value_grad, weight, 1, 1).astype(BF)
    hidden_grad = hidden_grad.reshape(seg, n_grp, n_leaf, own_rows).transpose(0, 2, 1, 3)
    hidden_grad = with_layout_constraint(
        hidden_grad.reshape(1, seg, depth), Layout(major_to_minor=(0, 1, 2))
    )

    fifth = swap(key_terms.reshape(-1, slots, DH))

    (key_sums,) = plain(
        key_kernel, [table, fifth], [shape((n_leaf, TILE, DH), BF)], totals, scalars=1
    )
    weight_part, hidden_grad, key_sums = lax.optimization_barrier(
        (weight_part, hidden_grad, key_sums)
    )

    (sixth,) = plain(
        functools.partial(join_kernel, own_rows),
        [key_sums, weight_part],
        [shape((n_leaf, TILE + tail, DH), BF)],
    )
    sixth = swap(sixth)
    key_grad, weight_grad = plain(
        functools.partial(last_kernel, own_rows),
        [sixth, key_term_own],
        [shape((seg, width), BF), shape((own_rows, width), F32)],
        [pltpu.VMEM((tail, DH), F32)],
    )
    return (output[None], query_grad[None], key_grad[None], hidden_grad, weight_grad)


def solution(mesh):
    rows = P("grp", "leaf", None)
    spread = P(("leaf", "grp"), None)
    return jax.shard_map(
        functools.partial(shards, mesh.shape["leaf"], mesh.shape["grp"]),
        mesh=mesh,
        in_specs=(rows, rows, rows, spread, P("grp", "leaf"), rows),
        out_specs=(rows, rows, rows, rows, spread),
        check_vma=False,
    )
```

```python
import functools

import jax
import jax.numpy as jnp
from jax import lax
from jax.experimental import pallas as pl
from jax.experimental.layout import Layout, with_layout_constraint
from jax.experimental.pallas import tpu as pltpu
from jax.sharding import PartitionSpec as P

HQ = 40
HK = 4
DH = 128
GROUPS = HQ // HK
SLOTS = 3
TILE = 16
LOG2E = 1.4426950408889634
BF = jnp.bfloat16
F32 = jnp.float32
VMEM_LIMIT = 28 * 1024 * 1024
ATTENTION_LIMIT = 56 * 1024 * 1024


def quotient(value, divisor, limit):
    shift = next(
        n
        for n in range(8, 20)
        if all(x * ((1 << n) // divisor + 1) >> n == x // divisor for x in range(limit))
    )
    return (value * ((1 << shift) // divisor + 1)) >> shift


def spread_rows(own_rows):
    count = HK * own_rows
    size = 8 * count
    target = lax.broadcasted_iota(jnp.int32, (size, size), 0)
    leaf = quotient(target, count, size)
    rest = target - leaf * count
    head = quotient(rest, own_rows, count)
    source = (head * 8 + leaf) * own_rows + (rest - head * own_rows)
    found = source == lax.broadcasted_iota(jnp.int32, (size, size), 1)
    return jnp.where(found, 1.0, 0.0).astype(BF)


def pack_kernel(own_rows, parent, keys, weight, sent, rows):
    count = HK * own_rows
    rows[...] = jnp.broadcast_to(parent[...].astype(F32), rows.shape)
    for head in range(HK):
        rows[head * own_rows : (head + 1) * own_rows, :] = weight[
            :, head * DH : (head + 1) * DH
        ].astype(F32)
    common = rows[...].astype(BF)
    for piece in range(sent.shape[0]):
        block, head = piece // HK, piece % HK
        sent[piece, 0:TILE, :] = keys[block * TILE : (block + 1) * TILE, head * DH : (head + 1) * DH]
        sent[piece, TILE:, :] = common


def weight_kernel(own_rows, held, weight):
    select = spread_rows(own_rows)
    count = HK * own_rows
    for group in range(held.shape[0] // 8):
        part = held[group * 8 : (group + 1) * 8, TILE:, :].astype(F32)[:, :count, :]
        part = part.reshape(8 * count, DH).astype(BF)
        moved = dot(select, part, 0, 0).astype(BF)
        for head in range(HK):
            weight[
                group * 8 * own_rows : (group + 1) * 8 * own_rows, head * DH : (head + 1) * DH
            ] = moved[head * 8 * own_rows : (head + 1) * 8 * own_rows, :]


def fetch_kernel(held, sent, table, wide, parents, arrived):
    nodes = held.shape[0]
    tail = held[:, held.shape[1] - TILE :, :].astype(F32)
    wide[...] = jnp.max(tail[:, TILE // 2 :, :], axis=1).astype(jnp.int32)
    copy = pltpu.make_async_copy(wide, parents, arrived)
    copy.start()
    for node in range(nodes):
        sent[node, 0:TILE, :] = held[0, 0:TILE, :]
    copy.wait()
    for node in range(nodes):
        parent = parents[node, 0]
        above = table[jnp.maximum(parent, 0)] if node > 0 else -1
        deep = jnp.logical_and(parent > 0, above >= 0)
        table[node] = jnp.where(deep, above, jnp.where(parent > 0, parent, -1))
        table[nodes + node] = jnp.where(deep, parent, -1)
    for node in range(nodes):
        for slot in range(1, SLOTS):
            owner = jnp.maximum(table[(slot - 1) * nodes + node], 0)
            sent[node, slot * TILE : (slot + 1) * TILE, :] = held[owner, 0:TILE, :]


def add_up(table, held, totals):
    nodes = held.shape[0]
    for total in totals:
        total[...] = jnp.zeros_like(total)
    root = jnp.zeros((TILE, DH), F32)
    for node in range(nodes):
        root = root + held[node, 0:TILE, :].astype(F32)
        for slot in range(1, SLOTS):
            owner = jnp.maximum(table[(slot - 1) * nodes + node], 0)
            totals[slot - 1][owner] += held[node, slot * TILE : (slot + 1) * TILE, :].astype(F32)
    totals[0][0] += root


def value_kernel(table, held, sent, *totals):
    nodes = held.shape[0]
    values = slice(SLOTS * TILE, (SLOTS + 1) * TILE)
    add_up(table, held, totals)
    for node in range(nodes):
        sent[node, 0:TILE, :] = held[0, values, :]
        for slot in range(1, SLOTS):
            owner = jnp.maximum(table[(slot - 1) * nodes + node], 0)
            sent[node, slot * TILE : (slot + 1) * TILE, :] = held[owner, values, :]
        sent[node, values, :] = (totals[0][node] + totals[1][node]).astype(BF)


def key_kernel(table, held, sums, *totals):
    add_up(table, held, totals)
    for node in range(held.shape[0]):
        sums[node] = (totals[0][node] + totals[1][node]).astype(BF)


def join_kernel(own_rows, sums, part, sent):
    select = spread_rows(own_rows)
    count = HK * own_rows
    sent[:, 0:TILE, :] = sums[...]
    for group in range(sent.shape[0] // 8):
        rows = part[group * 8 * own_rows : (group + 1) * 8 * own_rows, :]
        rows = jnp.concatenate([rows[:, h * DH : (h + 1) * DH] for h in range(HK)], axis=0)
        moved = dot(select, rows, 1, 0).reshape(8, count, DH)
        fill = jnp.zeros((8, sent.shape[1] - TILE - count, DH), F32)
        sent[group * 8 : (group + 1) * 8, TILE:, :] = jnp.concatenate(
            [moved, fill], axis=1
        ).astype(BF)


def last_kernel(own_rows, held, key_own, key_grad, weight_grad, rows):
    for piece in range(held.shape[0]):
        block, head = piece // HK, piece % HK
        at = (slice(block * TILE, (block + 1) * TILE), slice(head * DH, (head + 1) * DH))
        key_grad[at] = (held[piece, 0:TILE, :].astype(F32) + key_own[at].astype(F32)).astype(BF)
    rows[...] = jnp.sum(held[:, TILE:, :].astype(F32), axis=0)
    for head in range(HK):
        weight_grad[:, head * DH : (head + 1) * DH] = rows[
            head * own_rows : (head + 1) * own_rows, :
        ]


def plain(kernel, arrays, outs, scratch=(), scalars=0, scalar_outs=0, limit=VMEM_LIMIT):
    smem, vmem = pl.BlockSpec(memory_space=pltpu.SMEM), pl.BlockSpec(memory_space=pltpu.VMEM)
    moved = sum(a.size * a.dtype.itemsize for a in list(arrays) + list(outs))
    return pl.pallas_call(
        kernel,
        out_shape=outs,
        in_specs=[smem] * scalars + [vmem] * (len(arrays) - scalars),
        out_specs=[vmem] * (len(outs) - scalar_outs) + [smem] * scalar_outs,
        scratch_shapes=list(scratch),
        compiler_params=pltpu.CompilerParams(vmem_limit_bytes=limit),
        cost_estimate=pl.CostEstimate(flops=0, bytes_accessed=moved, transcendentals=0),
    )(*arrays)


def rows_of(pieces, own):
    parts = [
        pieces[:, 0, slot * TILE : (slot + 1) * TILE, :].reshape(-1, DH) for slot in range(SLOTS)
    ]
    return jnp.concatenate(parts + [own[...]], axis=0)


def put_rows(pieces, own, rows):
    seg = own.shape[0]
    for slot in range(SLOTS):
        block = rows[slot * seg : (slot + 1) * seg, :]
        pieces[:, 0, slot * TILE : (slot + 1) * TILE, :] = block.reshape(-1, TILE, DH).astype(BF)
    own[...] = rows[SLOTS * seg :, :].astype(BF)


def pair(block, index):
    return jnp.concatenate(
        [block[:, (2 * index + i) * DH : (2 * index + i + 1) * DH] for i in range(2)], axis=0
    )


def heads_of(block):
    return jnp.concatenate([block[:, i * DH : (i + 1) * DH] for i in range(GROUPS)], axis=0)


def put_pair(block, index, rows):
    seg = block.shape[0]
    for i in range(2):
        block[:, (2 * index + i) * DH : (2 * index + i + 1) * DH] = rows[
            i * seg : (i + 1) * seg, :
        ].astype(BF)


def dot(lhs, rhs, left, right):
    return lax.dot_general(lhs, rhs, (((left,), (right,)), ((), ())), preferred_element_type=F32)


def masks_of(present, bias):
    seg = bias.shape[0]

    @pl.when(pl.program_id(0) == 0)
    def _():
        key_ids = lax.broadcasted_iota(jnp.int32, bias.shape, 0)
        query_ids = lax.broadcasted_iota(jnp.int32, bias.shape, 1) % seg
        bias[...] = jnp.where(key_ids <= query_ids, 0.0, -1e30)

    return [jnp.where(present[slot] > 0, 0.0, -1e30).astype(F32) for slot in range(SLOTS)]


def scores_of(keys, queries, levels, bias):
    seg = bias.shape[0]
    scores = dot(keys, queries, 1, 1) * (LOG2E / DH**0.5)
    return jnp.concatenate(
        [scores[slot * seg : (slot + 1) * seg, :] + levels[slot] for slot in range(SLOTS)]
        + [scores[SLOTS * seg :, :] + bias[...]],
        axis=0,
    )


def probs_kernel(
    present, query, grad, key_pieces, key_own, probs, value_pieces, value_own, bias, low
):
    seg = query.shape[0]
    levels = masks_of(present, bias)
    keys = rows_of(key_pieces, key_own)
    for index in range(GROUPS // 2):
        at = slice(index * 2 * seg, (index + 1) * 2 * seg)
        scores = scores_of(keys, pair(query, index), levels, bias)
        weight = jnp.exp2(scores - jnp.max(scores, axis=0, keepdims=True))
        prob = weight * (1.0 / jnp.sum(weight, axis=0, keepdims=True))
        probs[0, :, at] = prob
        low[:, at] = prob.astype(BF)
    put_rows(value_pieces, value_own, dot(low[...], heads_of(grad), 1, 0))


def grads_kernel(
    query, grad, probs, key_pieces, key_own, value_pieces, value_own,
    output, query_grad, grad_pieces, grad_own, low,
):
    seg = query.shape[0]
    keys = rows_of(key_pieces, key_own)
    values = rows_of(value_pieces, value_own)
    keys_t, values_t = keys.T, values.T
    for index in range(GROUPS // 2):
        at = slice(index * 2 * seg, (index + 1) * 2 * seg)
        prob = probs[0, :, at]
        dprob = dot(values, pair(grad, index), 1, 1)
        delta = jnp.sum(prob * dprob, axis=0, keepdims=True)
        dscore = (prob * (dprob - delta)).astype(BF)
        low[:, at] = dscore
        put_pair(output, index, dot(values_t, prob.astype(BF), 1, 0).astype(BF).T)
        put_pair(query_grad, index, (dot(keys_t, dscore, 1, 0) * (1.0 / DH**0.5)).astype(BF).T)
    total = dot(low[...], heads_of(query), 1, 0)
    put_rows(grad_pieces, grad_own, total * (1.0 / DH**0.5))


def attention(
    kernel, lead, arrays, outs, scratch, flops, transcendentals, start=0, stop=HK, into=()
):
    def spec(shape):
        if len(shape) == 4:
            return pl.BlockSpec((shape[0], 1) + shape[2:], lambda h: (0, h + start, 0, 0))
        if len(shape) == 3:
            return pl.BlockSpec((1,) + shape[1:], lambda h: (h + start, 0, 0))
        return pl.BlockSpec((shape[0], shape[1] // HK), lambda h: (0, h + start))

    given = len(lead) + len(arrays)

    def run(*refs):
        kernel(*refs[:given], *refs[given + len(into) :])

    moved = sum(a.size * a.dtype.itemsize for a in arrays) + sum(
        o.size * o.dtype.itemsize for o in outs
    )
    return pl.pallas_call(
        run,
        grid=(stop - start,),
        out_shape=outs,
        in_specs=[pl.BlockSpec(memory_space=pltpu.SMEM)] * len(lead)
        + [spec(a.shape) for a in arrays]
        + [pl.BlockSpec(memory_space=pl.ANY)] * len(into),
        input_output_aliases={given + i: i for i in range(len(into))},
        out_specs=[spec(o.shape) for o in outs],
        scratch_shapes=scratch,
        compiler_params=pltpu.CompilerParams(vmem_limit_bytes=ATTENTION_LIMIT),
        cost_estimate=pl.CostEstimate(
            flops=flops * (stop - start) // HK,
            bytes_accessed=moved * (stop - start) // HK,
            transcendentals=transcendentals * (stop - start) // HK,
        ),
    )(*lead, *arrays, *into)


def share_kernel(which, pieces, own, columns, value_grad, part):
    @pl.when(pl.program_id(0) == 0)
    def _():
        for block in range(pieces.shape[0]):
            for head in range(HK):
                at = (slice(block * TILE, (block + 1) * TILE), slice(head * DH, (head + 1) * DH))
                value_grad[at] = (
                    pieces[block, head].astype(F32) + own[at].astype(F32)
                ).astype(BF)

    part[...] = dot(columns[...], value_grad[...], 1, 0).astype(BF)


def combine_kernel(which, value_grad, columns, arrived, part):
    own = dot(columns[...], value_grad[...], 1, 0)
    part[...] = (own + arrived[...].astype(F32)).astype(BF)


def share(kernel, which, first, columns, rest, outs, n_grp):
    rows = columns.shape[0] // n_grp

    def spec(shape):
        if len(shape) == 4:
            return pl.BlockSpec(shape[:2] + (TILE, DH), lambda i, which: (0, 0, SLOTS, 0))
        if shape[0] == columns.shape[1]:
            return pl.BlockSpec(shape, lambda i, which: (0, 0))
        return pl.BlockSpec((rows, shape[1]), lambda i, which: (i, 0))

    return pl.pallas_call(
        kernel,
        out_shape=outs,
        grid_spec=pltpu.PrefetchScalarGridSpec(
            num_scalar_prefetch=1,
            grid=(n_grp // 2,),
            in_specs=[spec(a.shape) for a in first]
            + [pl.BlockSpec((rows, columns.shape[1]), lambda i, which: (2 * i + which[0], 0))]
            + [spec(a.shape) for a in rest],
            out_specs=[spec(o.shape) for o in outs],
        ),
        compiler_params=pltpu.CompilerParams(vmem_limit_bytes=VMEM_LIMIT),
        cost_estimate=pl.CostEstimate(
            flops=columns.size * 512, bytes_accessed=columns.size * 5, transcendentals=0
        ),
    )(which, *first, columns, *rest)


def to_pieces(rows):
    seg, width = rows.shape
    split = rows.reshape(seg // TILE, TILE, width // DH, DH).transpose(0, 2, 1, 3)
    return split.reshape(-1, TILE, DH)


def swap(array):
    return lax.all_to_all(array, "leaf", 0, 0, tiled=True)


def shards(n_leaf, n_grp, hidden_states, query_rows, key_rows, value_weight, parent_links, out_grad):
    hidden, query, keys, grad = hidden_states[0], query_rows[0], key_rows[0], out_grad[0]
    seg, width = keys.shape
    depth = hidden.shape[1]
    own_rows = value_weight.shape[0]
    blocks = seg // TILE
    tail = -(-(HK * own_rows + TILE // 2) // TILE) * TILE
    shape = jax.ShapeDtypeStruct
    flops = 2 * seg * 4 * seg * DH * HQ
    totals = [pltpu.VMEM((n_leaf, TILE, DH), F32)] * (SLOTS - 1)
    slots = SLOTS * TILE

    columns = hidden.T.reshape(n_leaf, n_grp, own_rows, seg).transpose(1, 0, 2, 3)
    columns = columns.reshape(depth, seg)
    core = lax.axis_index("grp").astype(jnp.int32).reshape(1) % 2

    (first,) = plain(
        functools.partial(pack_kernel, own_rows),
        [parent_links, keys, value_weight],
        [shape((n_leaf, TILE + tail, DH), BF)],
        [pltpu.VMEM((tail, DH), F32)],
        limit=ATTENTION_LIMIT,
    )
    first = swap(first)

    (weight,) = plain(
        functools.partial(weight_kernel, own_rows),
        [first],
        [shape((n_leaf * own_rows, width), BF)],
    )
    weight = lax.all_gather(weight, "grp", axis=0, tiled=True)
    second, table = plain(
        fetch_kernel,
        [first],
        [shape((n_leaf, slots, DH), BF), shape(((SLOTS - 1) * n_leaf,), jnp.int32)],
        [
            pltpu.VMEM((n_leaf, DH), jnp.int32),
            pltpu.SMEM((n_leaf, DH), jnp.int32),
            pltpu.SemaphoreType.DMA,
        ],
        scalar_outs=1,
    )
    key_pieces = swap(second).reshape(blocks, HK, slots, DH)
    own = lax.axis_index("leaf")
    here = (table.reshape(SLOTS - 1, n_leaf) >= 0) & (jnp.arange(n_leaf) == own)
    present = jnp.concatenate([(own > 0)[None], jnp.any(here, axis=1)]).astype(jnp.int32)
    probs, value_terms, value_term_own = attention(
        probs_kernel,
        [present],
        [query, grad, key_pieces, keys],
        [
            shape((HK, 4 * seg, GROUPS * seg), F32),
            shape((blocks, HK, slots, DH), BF),
            shape((seg, width), BF),
        ],
        [pltpu.VMEM((seg, 2 * seg), F32), pltpu.VMEM((4 * seg, GROUPS * seg), BF)],
        2 * flops,
        HQ * seg * 4 * seg,
    )

    values = dot(columns, weight, 0, 0).astype(BF)
    third = jnp.concatenate([value_terms.reshape(-1, slots, DH), to_pieces(values)], axis=1)
    third = swap(third)

    (fourth,) = plain(
        value_kernel, [table, third], [shape((n_leaf, slots + TILE, DH), BF)], totals, scalars=1
    )
    fourth = swap(fourth).reshape(blocks, HK, slots + TILE, DH)
    half = shape((depth // 2, width), BF)
    value_grad, weight_part = share(
        share_kernel,
        1 - core,
        [fourth, value_term_own],
        columns,
        [],
        [shape((seg, width), BF), half],
        n_grp,
    )
    weight_part = lax.ppermute(weight_part, "grp", [(i, i ^ 1) for i in range(n_grp)])
    backward = functools.partial(
        attention,
        grads_kernel,
        [],
        [query, grad, probs, key_pieces, keys, fourth, values],
        [
            shape((seg, HQ * DH), BF),
            shape((seg, HQ * DH), BF),
            shape((blocks, HK, slots, DH), BF),
            shape((seg, width), BF),
        ],
        [pltpu.VMEM((4 * seg, GROUPS * seg), BF)],
        4 * flops,
        0,
    )
    weight_part, *grads = lax.optimization_barrier((weight_part, *backward(stop=HK // 2)))
    (weight_part,) = share(
        combine_kernel, core, [value_grad], columns, [weight_part], [half], n_grp
    )
    weight_part = lax.psum_scatter(
        weight_part,
        "grp",
        scatter_dimension=0,
        axis_index_groups=[list(range(c, n_grp, 2)) for c in range(2)],
        tiled=True,
    )
    output, query_grad, key_terms, key_term_own = backward(start=HK // 2, into=grads)
    hidden_grad = dot(value_grad, weight, 1, 1).astype(BF)
    hidden_grad = hidden_grad.reshape(seg, n_grp, n_leaf, own_rows).transpose(0, 2, 1, 3)
    hidden_grad = with_layout_constraint(
        hidden_grad.reshape(1, seg, depth), Layout(major_to_minor=(0, 1, 2))
    )

    fifth = swap(key_terms.reshape(-1, slots, DH))

    (key_sums,) = plain(
        key_kernel, [table, fifth], [shape((n_leaf, TILE, DH), BF)], totals, scalars=1
    )
    weight_part, hidden_grad, key_sums = lax.optimization_barrier(
        (weight_part, hidden_grad, key_sums)
    )

    (sixth,) = plain(
        functools.partial(join_kernel, own_rows),
        [key_sums, weight_part],
        [shape((n_leaf, TILE + tail, DH), BF)],
    )
    sixth = swap(sixth)
    key_grad, weight_grad = plain(
        functools.partial(last_kernel, own_rows),
        [sixth, key_term_own],
        [shape((seg, width), BF), shape((own_rows, width), F32)],
        [pltpu.VMEM((tail, DH), F32)],
    )
    return (output[None], query_grad[None], key_grad[None], hidden_grad, weight_grad)


def solution(mesh):
    rows = P("grp", "leaf", None)
    spread = P(("leaf", "grp"), None)
    return jax.shard_map(
        functools.partial(shards, mesh.shape["leaf"], mesh.shape["grp"]),
        mesh=mesh,
        in_specs=(rows, rows, rows, spread, P("grp", "leaf"), rows),
        out_specs=(rows, rows, rows, rows, spread),
        check_vma=False,
    )
```

```python
import functools

import jax
import jax.numpy as jnp
from jax import lax
from jax.experimental import pallas as pl
from jax.experimental.layout import Layout, with_layout_constraint
from jax.experimental.pallas import tpu as pltpu
from jax.sharding import PartitionSpec as P

HQ = 40
HK = 4
DH = 128
GROUPS = HQ // HK
SLOTS = 3
TILE = 16
LOG2E = 1.4426950408889634
BF = jnp.bfloat16
F32 = jnp.float32
VMEM_LIMIT = 28 * 1024 * 1024
ATTENTION_LIMIT = 56 * 1024 * 1024


def quotient(value, divisor, limit):
    shift = next(
        n
        for n in range(8, 20)
        if all(x * ((1 << n) // divisor + 1) >> n == x // divisor for x in range(limit))
    )
    return (value * ((1 << shift) // divisor + 1)) >> shift


def spread_rows(own_rows):
    count = HK * own_rows
    size = 8 * count
    target = lax.broadcasted_iota(jnp.int32, (size, size), 0)
    leaf = quotient(target, count, size)
    rest = target - leaf * count
    head = quotient(rest, own_rows, count)
    source = (head * 8 + leaf) * own_rows + (rest - head * own_rows)
    found = source == lax.broadcasted_iota(jnp.int32, (size, size), 1)
    return jnp.where(found, 1.0, 0.0).astype(BF)


def pack_kernel(own_rows, parent, keys, weight, sent, rows):
    count = HK * own_rows
    rows[...] = jnp.broadcast_to(parent[...].astype(F32), rows.shape)
    for head in range(HK):
        rows[head * own_rows : (head + 1) * own_rows, :] = weight[
            :, head * DH : (head + 1) * DH
        ].astype(F32)
    common = rows[...].astype(BF)
    for piece in range(sent.shape[0]):
        block, head = piece // HK, piece % HK
        sent[piece, 0:TILE, :] = keys[block * TILE : (block + 1) * TILE, head * DH : (head + 1) * DH]
        sent[piece, TILE:, :] = common


def weight_kernel(own_rows, held, weight):
    select = spread_rows(own_rows)
    count = HK * own_rows
    for group in range(held.shape[0] // 8):
        part = held[group * 8 : (group + 1) * 8, TILE:, :].astype(F32)[:, :count, :]
        part = part.reshape(8 * count, DH).astype(BF)
        moved = dot(select, part, 0, 0).astype(BF)
        for head in range(HK):
            weight[
                group * 8 * own_rows : (group + 1) * 8 * own_rows, head * DH : (head + 1) * DH
            ] = moved[head * 8 * own_rows : (head + 1) * 8 * own_rows, :]


def fetch_kernel(held, sent, table, wide, parents, arrived):
    nodes = held.shape[0]
    tail = held[:, held.shape[1] - TILE :, :].astype(F32)
    wide[...] = jnp.max(tail[:, TILE // 2 :, :], axis=1).astype(jnp.int32)
    copy = pltpu.make_async_copy(wide, parents, arrived)
    copy.start()
    for node in range(nodes):
        sent[node, 0:TILE, :] = held[0, 0:TILE, :]
    copy.wait()
    for node in range(nodes):
        parent = parents[node, 0]
        above = table[jnp.maximum(parent, 0)] if node > 0 else -1
        deep = jnp.logical_and(parent > 0, above >= 0)
        table[node] = jnp.where(deep, above, jnp.where(parent > 0, parent, -1))
        table[nodes + node] = jnp.where(deep, parent, -1)
    for node in range(nodes):
        for slot in range(1, SLOTS):
            owner = jnp.maximum(table[(slot - 1) * nodes + node], 0)
            sent[node, slot * TILE : (slot + 1) * TILE, :] = held[owner, 0:TILE, :]


def add_up(table, held, totals):
    nodes = held.shape[0]
    for total in totals:
        total[...] = jnp.zeros_like(total)
    root = jnp.zeros((TILE, DH), F32)
    for node in range(nodes):
        root = root + held[node, 0:TILE, :].astype(F32)
        for slot in range(1, SLOTS):
            owner = jnp.maximum(table[(slot - 1) * nodes + node], 0)
            totals[slot - 1][owner] += held[node, slot * TILE : (slot + 1) * TILE, :].astype(F32)
    totals[0][0] += root


def value_kernel(table, held, sent, *totals):
    nodes = held.shape[0]
    values = slice(SLOTS * TILE, (SLOTS + 1) * TILE)
    add_up(table, held, totals)
    for node in range(nodes):
        sent[node, 0:TILE, :] = held[0, values, :]
        for slot in range(1, SLOTS):
            owner = jnp.maximum(table[(slot - 1) * nodes + node], 0)
            sent[node, slot * TILE : (slot + 1) * TILE, :] = held[owner, values, :]
        sent[node, values, :] = (totals[0][node] + totals[1][node]).astype(BF)


def key_kernel(table, held, sums, *totals):
    add_up(table, held, totals)
    for node in range(held.shape[0]):
        sums[node] = (totals[0][node] + totals[1][node]).astype(BF)


def join_kernel(own_rows, sums, part, sent):
    select = spread_rows(own_rows)
    count = HK * own_rows
    sent[:, 0:TILE, :] = sums[...]
    for group in range(sent.shape[0] // 8):
        rows = part[group * 8 * own_rows : (group + 1) * 8 * own_rows, :]
        rows = jnp.concatenate([rows[:, h * DH : (h + 1) * DH] for h in range(HK)], axis=0)
        moved = dot(select, rows, 1, 0).reshape(8, count, DH)
        fill = jnp.zeros((8, sent.shape[1] - TILE - count, DH), F32)
        sent[group * 8 : (group + 1) * 8, TILE:, :] = jnp.concatenate(
            [moved, fill], axis=1
        ).astype(BF)


def last_kernel(own_rows, held, key_own, key_grad, weight_grad, rows):
    for piece in range(held.shape[0]):
        block, head = piece // HK, piece % HK
        at = (slice(block * TILE, (block + 1) * TILE), slice(head * DH, (head + 1) * DH))
        key_grad[at] = (held[piece, 0:TILE, :].astype(F32) + key_own[at].astype(F32)).astype(BF)
    rows[...] = jnp.sum(held[:, TILE:, :].astype(F32), axis=0)
    for head in range(HK):
        weight_grad[:, head * DH : (head + 1) * DH] = rows[
            head * own_rows : (head + 1) * own_rows, :
        ]


def plain(kernel, arrays, outs, scratch=(), scalars=0, scalar_outs=0, limit=VMEM_LIMIT):
    smem, vmem = pl.BlockSpec(memory_space=pltpu.SMEM), pl.BlockSpec(memory_space=pltpu.VMEM)
    moved = sum(a.size * a.dtype.itemsize for a in list(arrays) + list(outs))
    return pl.pallas_call(
        kernel,
        out_shape=outs,
        in_specs=[smem] * scalars + [vmem] * (len(arrays) - scalars),
        out_specs=[vmem] * (len(outs) - scalar_outs) + [smem] * scalar_outs,
        scratch_shapes=list(scratch),
        compiler_params=pltpu.CompilerParams(vmem_limit_bytes=limit),
        cost_estimate=pl.CostEstimate(flops=0, bytes_accessed=moved, transcendentals=0),
    )(*arrays)


def rows_of(pieces, own):
    parts = [
        pieces[:, 0, slot * TILE : (slot + 1) * TILE, :].reshape(-1, DH) for slot in range(SLOTS)
    ]
    return jnp.concatenate(parts + [own[...]], axis=0)


def put_rows(pieces, own, rows):
    seg = own.shape[0]
    for slot in range(SLOTS):
        block = rows[slot * seg : (slot + 1) * seg, :]
        pieces[:, 0, slot * TILE : (slot + 1) * TILE, :] = block.reshape(-1, TILE, DH).astype(BF)
    own[...] = rows[SLOTS * seg :, :].astype(BF)


def pair(block, index):
    return jnp.concatenate(
        [block[:, (2 * index + i) * DH : (2 * index + i + 1) * DH] for i in range(2)], axis=0
    )


def heads_of(block):
    return jnp.concatenate([block[:, i * DH : (i + 1) * DH] for i in range(GROUPS)], axis=0)


def put_pair(block, index, rows):
    seg = block.shape[0]
    for i in range(2):
        block[:, (2 * index + i) * DH : (2 * index + i + 1) * DH] = rows[
            i * seg : (i + 1) * seg, :
        ].astype(BF)


def dot(lhs, rhs, left, right):
    return lax.dot_general(lhs, rhs, (((left,), (right,)), ((), ())), preferred_element_type=F32)


def masks_of(present, bias):
    seg = bias.shape[0]

    @pl.when(pl.program_id(0) == 0)
    def _():
        key_ids = lax.broadcasted_iota(jnp.int32, bias.shape, 0)
        query_ids = lax.broadcasted_iota(jnp.int32, bias.shape, 1) % seg
        bias[...] = jnp.where(key_ids <= query_ids, 0.0, -1e30)

    return [jnp.where(present[slot] > 0, 0.0, -1e30).astype(F32) for slot in range(SLOTS)]


def scores_of(keys, queries, levels, bias):
    seg = bias.shape[0]
    scores = dot(keys, queries, 1, 1) * (LOG2E / DH**0.5)
    return jnp.concatenate(
        [scores[slot * seg : (slot + 1) * seg, :] + levels[slot] for slot in range(SLOTS)]
        + [scores[SLOTS * seg :, :] + bias[...]],
        axis=0,
    )


def probs_kernel(
    present, query, grad, key_pieces, key_own, probs, value_pieces, value_own, bias
):
    seg = query.shape[0]
    levels = masks_of(present, bias)
    keys = rows_of(key_pieces, key_own)
    for index in range(GROUPS // 2):
        at = slice(index * 2 * seg, (index + 1) * 2 * seg)
        scores = scores_of(keys, pair(query, index), levels, bias)
        weight = jnp.exp2(scores - jnp.max(scores, axis=0, keepdims=True))
        prob = weight * (1.0 / jnp.sum(weight, axis=0, keepdims=True))
        probs[0, :, at] = prob.astype(BF)
    put_rows(value_pieces, value_own, dot(probs[0], heads_of(grad), 1, 0))


def grads_kernel(
    query, grad, probs, key_pieces, key_own, value_pieces, value_own,
    output, query_grad, grad_pieces, grad_own, low,
):
    seg = query.shape[0]
    keys = rows_of(key_pieces, key_own)
    values = rows_of(value_pieces, value_own)
    keys_t, values_t = keys.T, values.T
    for index in range(GROUPS // 2):
        at = slice(index * 2 * seg, (index + 1) * 2 * seg)
        prob_low = probs[0, :, at]
        prob = prob_low.astype(F32)
        dprob = dot(values, pair(grad, index), 1, 1)
        delta = jnp.sum(prob * dprob, axis=0, keepdims=True) / jnp.sum(prob, axis=0, keepdims=True)
        dscore = (prob * (dprob - delta)).astype(BF)
        low[:, at] = dscore
        put_pair(output, index, dot(values_t, prob_low, 1, 0).astype(BF).T)
        put_pair(query_grad, index, (dot(keys_t, dscore, 1, 0) * (1.0 / DH**0.5)).astype(BF).T)
    total = dot(low[...], heads_of(query), 1, 0)
    put_rows(grad_pieces, grad_own, total * (1.0 / DH**0.5))


def attention(
    kernel, lead, arrays, outs, scratch, flops, transcendentals, start=0, stop=HK, into=()
):
    def spec(shape):
        if len(shape) == 4:
            return pl.BlockSpec((shape[0], 1) + shape[2:], lambda h: (0, h + start, 0, 0))
        if len(shape) == 3:
            return pl.BlockSpec((1,) + shape[1:], lambda h: (h + start, 0, 0))
        return pl.BlockSpec((shape[0], shape[1] // HK), lambda h: (0, h + start))

    given = len(lead) + len(arrays)

    def run(*refs):
        kernel(*refs[:given], *refs[given + len(into) :])

    moved = sum(a.size * a.dtype.itemsize for a in arrays) + sum(
        o.size * o.dtype.itemsize for o in outs
    )
    return pl.pallas_call(
        run,
        grid=(stop - start,),
        out_shape=outs,
        in_specs=[pl.BlockSpec(memory_space=pltpu.SMEM)] * len(lead)
        + [spec(a.shape) for a in arrays]
        + [pl.BlockSpec(memory_space=pl.ANY)] * len(into),
        input_output_aliases={given + i: i for i in range(len(into))},
        out_specs=[spec(o.shape) for o in outs],
        scratch_shapes=scratch,
        compiler_params=pltpu.CompilerParams(vmem_limit_bytes=ATTENTION_LIMIT),
        cost_estimate=pl.CostEstimate(
            flops=flops * (stop - start) // HK,
            bytes_accessed=moved * (stop - start) // HK,
            transcendentals=transcendentals * (stop - start) // HK,
        ),
    )(*lead, *arrays, *into)


def share_kernel(which, pieces, own, columns, value_grad, part):
    @pl.when(pl.program_id(0) == 0)
    def _():
        for block in range(pieces.shape[0]):
            for head in range(HK):
                at = (slice(block * TILE, (block + 1) * TILE), slice(head * DH, (head + 1) * DH))
                value_grad[at] = (
                    pieces[block, head].astype(F32) + own[at].astype(F32)
                ).astype(BF)

    part[...] = dot(columns[...], value_grad[...], 1, 0).astype(BF)


def combine_kernel(which, value_grad, columns, arrived, part):
    own = dot(columns[...], value_grad[...], 1, 0)
    part[...] = (own + arrived[...].astype(F32)).astype(BF)


def share(kernel, which, first, columns, rest, outs, n_grp):
    rows = columns.shape[0] // n_grp

    def spec(shape):
        if len(shape) == 4:
            return pl.BlockSpec(shape[:2] + (TILE, DH), lambda i, which: (0, 0, SLOTS, 0))
        if shape[0] == columns.shape[1]:
            return pl.BlockSpec(shape, lambda i, which: (0, 0))
        return pl.BlockSpec((rows, shape[1]), lambda i, which: (i, 0))

    return pl.pallas_call(
        kernel,
        out_shape=outs,
        grid_spec=pltpu.PrefetchScalarGridSpec(
            num_scalar_prefetch=1,
            grid=(n_grp // 2,),
            in_specs=[spec(a.shape) for a in first]
            + [pl.BlockSpec((rows, columns.shape[1]), lambda i, which: (2 * i + which[0], 0))]
            + [spec(a.shape) for a in rest],
            out_specs=[spec(o.shape) for o in outs],
        ),
        compiler_params=pltpu.CompilerParams(vmem_limit_bytes=VMEM_LIMIT),
        cost_estimate=pl.CostEstimate(
            flops=columns.size * 512, bytes_accessed=columns.size * 5, transcendentals=0
        ),
    )(which, *first, columns, *rest)


def to_pieces(rows):
    seg, width = rows.shape
    split = rows.reshape(seg // TILE, TILE, width // DH, DH).transpose(0, 2, 1, 3)
    return split.reshape(-1, TILE, DH)


def swap(array):
    return lax.all_to_all(array, "leaf", 0, 0, tiled=True)


def shards(n_leaf, n_grp, hidden_states, query_rows, key_rows, value_weight, parent_links, out_grad):
    hidden, query, keys, grad = hidden_states[0], query_rows[0], key_rows[0], out_grad[0]
    seg, width = keys.shape
    depth = hidden.shape[1]
    own_rows = value_weight.shape[0]
    blocks = seg // TILE
    tail = -(-(HK * own_rows + TILE // 2) // TILE) * TILE
    shape = jax.ShapeDtypeStruct
    flops = 2 * seg * 4 * seg * DH * HQ
    totals = [pltpu.VMEM((n_leaf, TILE, DH), F32)] * (SLOTS - 1)
    slots = SLOTS * TILE

    columns = hidden.T.reshape(n_leaf, n_grp, own_rows, seg).transpose(1, 0, 2, 3)
    columns = columns.reshape(depth, seg)
    core = lax.axis_index("grp").astype(jnp.int32).reshape(1) % 2

    (first,) = plain(
        functools.partial(pack_kernel, own_rows),
        [parent_links, keys, value_weight],
        [shape((n_leaf, TILE + tail, DH), BF)],
        [pltpu.VMEM((tail, DH), F32)],
        limit=ATTENTION_LIMIT,
    )
    first = swap(first)

    (weight,) = plain(
        functools.partial(weight_kernel, own_rows),
        [first],
        [shape((n_leaf * own_rows, width), BF)],
    )
    weight = lax.all_gather(weight, "grp", axis=0, tiled=True)
    second, table = plain(
        fetch_kernel,
        [first],
        [shape((n_leaf, slots, DH), BF), shape(((SLOTS - 1) * n_leaf,), jnp.int32)],
        [
            pltpu.VMEM((n_leaf, DH), jnp.int32),
            pltpu.SMEM((n_leaf, DH), jnp.int32),
            pltpu.SemaphoreType.DMA,
        ],
        scalar_outs=1,
    )
    key_pieces = swap(second).reshape(blocks, HK, slots, DH)
    own = lax.axis_index("leaf")
    here = (table.reshape(SLOTS - 1, n_leaf) >= 0) & (jnp.arange(n_leaf) == own)
    present = jnp.concatenate([(own > 0)[None], jnp.any(here, axis=1)]).astype(jnp.int32)
    probs, value_terms, value_term_own = attention(
        probs_kernel,
        [present],
        [query, grad, key_pieces, keys],
        [
            shape((HK, 4 * seg, GROUPS * seg), BF),
            shape((blocks, HK, slots, DH), BF),
            shape((seg, width), BF),
        ],
        [pltpu.VMEM((seg, 2 * seg), F32)],
        2 * flops,
        HQ * seg * 4 * seg,
    )

    values = dot(columns, weight, 0, 0).astype(BF)
    third = jnp.concatenate([value_terms.reshape(-1, slots, DH), to_pieces(values)], axis=1)
    third = swap(third)

    (fourth,) = plain(
        value_kernel, [table, third], [shape((n_leaf, slots + TILE, DH), BF)], totals, scalars=1
    )
    fourth = swap(fourth).reshape(blocks, HK, slots + TILE, DH)
    half = shape((depth // 2, width), BF)
    value_grad, weight_part = share(
        share_kernel,
        1 - core,
        [fourth, value_term_own],
        columns,
        [],
        [shape((seg, width), BF), half],
        n_grp,
    )
    weight_part = lax.ppermute(weight_part, "grp", [(i, i ^ 1) for i in range(n_grp)])
    backward = functools.partial(
        attention,
        grads_kernel,
        [],
        [query, grad, probs, key_pieces, keys, fourth, values],
        [
            shape((seg, HQ * DH), BF),
            shape((seg, HQ * DH), BF),
            shape((blocks, HK, slots, DH), BF),
            shape((seg, width), BF),
        ],
        [pltpu.VMEM((4 * seg, GROUPS * seg), BF)],
        4 * flops,
        0,
    )
    weight_part, *grads = lax.optimization_barrier((weight_part, *backward(stop=HK // 2)))
    (weight_part,) = share(
        combine_kernel, core, [value_grad], columns, [weight_part], [half], n_grp
    )
    weight_part = lax.psum_scatter(
        weight_part,
        "grp",
        scatter_dimension=0,
        axis_index_groups=[list(range(c, n_grp, 2)) for c in range(2)],
        tiled=True,
    )
    output, query_grad, key_terms, key_term_own = backward(start=HK // 2, into=grads)
    hidden_grad = dot(value_grad, weight, 1, 1).astype(BF)
    hidden_grad = hidden_grad.reshape(seg, n_grp, n_leaf, own_rows).transpose(0, 2, 1, 3)
    hidden_grad = with_layout_constraint(
        hidden_grad.reshape(1, seg, depth), Layout(major_to_minor=(0, 1, 2))
    )

    fifth = swap(key_terms.reshape(-1, slots, DH))

    (key_sums,) = plain(
        key_kernel, [table, fifth], [shape((n_leaf, TILE, DH), BF)], totals, scalars=1
    )
    weight_part, hidden_grad, key_sums = lax.optimization_barrier(
        (weight_part, hidden_grad, key_sums)
    )

    (sixth,) = plain(
        functools.partial(join_kernel, own_rows),
        [key_sums, weight_part],
        [shape((n_leaf, TILE + tail, DH), BF)],
    )
    sixth = swap(sixth)
    key_grad, weight_grad = plain(
        functools.partial(last_kernel, own_rows),
        [sixth, key_term_own],
        [shape((seg, width), BF), shape((own_rows, width), F32)],
        [pltpu.VMEM((tail, DH), F32)],
    )
    return (output[None], query_grad[None], key_grad[None], hidden_grad, weight_grad)


def solution(mesh):
    rows = P("grp", "leaf", None)
    spread = P(("leaf", "grp"), None)
    return jax.shard_map(
        functools.partial(shards, mesh.shape["leaf"], mesh.shape["grp"]),
        mesh=mesh,
        in_specs=(rows, rows, rows, spread, P("grp", "leaf"), rows),
        out_specs=(rows, rows, rows, rows, spread),
        check_vma=False,
    )
```
